128 devices in a mesh: wide: 8 (over x, core), narrow: 16 (over y, z).
Axes of the slice: x: 4, y: 4, z: 4, core: 2. Of those that a mesh axis runs over, the one named last changes fastest.
Arguments:
- blocks: float32 [5120, 256, 256], P(('wide', 'narrow'))
- block_map: int32 [5120, 2], P(('wide', 'narrow')), may hold values from 0 to 191, as said below
Outputs:
- factored: float32 [5120, 256, 256], P(('wide', 'narrow'))
The draws below stay inside these ranges and needn't reach their ends.
Inputs may be any that keep to these rules, and one draw needn't show every extreme that they name: `block_map`: each row names a block (r, c) with r >= c, and no block is named twice. The device at wide index w and narrow index n holds only blocks with r equal to n modulo the size of narrow and c equal to w modulo the size of wide. Block column 0 and block column 1 are held at wide index 0 and 1, 4 blocks of them on each device there, in that device's first 4 slots in ascending r; block column 0 holds the block (1, 0).
All inputs are finite; a program needn't handle non-finite values.
Results may differ from the reference program's by a relative error of at most 0.00005.
Values sent between devices are 32-bit elements; how exact they have to be, the bound alone decides.
A program may use at most 128 MiB of HBM per device.

```python
import jax
import jax.numpy as jnp
from jax import lax

W = 256
PR_DEV = 4
BLOCK_ROWS = 192
PANEL_ROWS = 64
BLK_DEV = 40
N_WIDE = 8
N_NARROW = 16


def panel_structure(key):
    per_class = BLOCK_ROWS // N_NARROW
    jitter = jax.random.randint(jax.random.fold_in(key, 11), (N_NARROW, per_class), 0, 1024)
    depth_index = jnp.arange(per_class, dtype=jnp.int32)[None, :]
    residue = jnp.arange(N_NARROW, dtype=jnp.int32)[:, None]
    priority = jnp.where((residue < 2) & (depth_index == 0), -1, jitter * 512 + depth_index)
    unused, picked = lax.top_k(priority, PR_DEV)
    chosen = residue + N_NARROW * picked.astype(jnp.int32)
    leading = jnp.concatenate([residue, chosen[:, :PR_DEV - 1]], axis=1)
    first_rows = jnp.sort(jnp.where(residue < 2, leading, chosen), axis=1)
    second_rows = jnp.sort(jnp.where(residue == 1, leading, chosen), axis=1)
    return (first_rows, second_rows)


def slot_layout(key):
    first_rows, second_rows = panel_structure(key)
    per_class = BLOCK_ROWS // N_NARROW
    per_wide = BLOCK_ROWS // N_WIDE
    member = jnp.zeros((BLOCK_ROWS,), jnp.int32).at[second_rows.reshape(-1)].set(1).at[1].set(0)
    big_step = 2 ** 22

    def device_slots(device):
        wide_pos = device // N_NARROW
        narrow_pos = device % N_NARROW
        own_key = jax.random.fold_in(jax.random.fold_in(key, 101), device)
        depth_index = jnp.arange(per_class, dtype=jnp.int32)[:, None]
        across = jnp.arange(per_wide, dtype=jnp.int32)[None, :]
        row_id = jnp.broadcast_to(narrow_pos + N_NARROW * depth_index, (per_class, per_wide))
        col_id = jnp.broadcast_to(wide_pos + N_WIDE * across, (per_class, per_wide))
        own_rows = jnp.where(wide_pos == 0, first_rows[narrow_pos], second_rows[narrow_pos])
        in_panel = (wide_pos < 2) & (across == 0) & jnp.any(row_id[:, :, None] == own_rows[None, None, :], axis=2)
        lower_part = (row_id >= col_id) & (col_id >= 2)
        pattern = lower_part & (member[row_id] == 1) & (member[col_id] == 1)
        jitter = jax.random.randint(own_key, (per_class, per_wide), 0, 256) * 2048 + depth_index * per_wide + across
        priority = jnp.where(in_panel, 3 * big_step + per_class - depth_index, jnp.where(pattern, 2 * big_step + jitter, jnp.where(lower_part & (depth_index == per_class - 1), big_step + 2 ** 21 + jitter, jnp.where(lower_part, big_step + jitter, jitter))))
        unused, picked = lax.top_k(priority.reshape(-1), BLK_DEV)
        return jnp.stack([row_id.reshape(-1)[picked], col_id.reshape(-1)[picked]], axis=1)
    layouts = jax.vmap(device_slots)(jnp.arange(N_WIDE * N_NARROW, dtype=jnp.int32))
    return layouts.reshape(-1, 2)


def draw_block_map(key, part):
    return slot_layout(key).astype(jnp.int32)


def draw_blocks(key, part):
    layout = slot_layout(key)
    on_diag = (layout[:, 0] == layout[:, 1])[:, None, None]
    slot_total = layout.shape[0]
    off_part = 0.03 * jax.random.truncated_normal(jax.random.fold_in(key, 33), -3.0, 3.0, (slot_total, W, W), jnp.float32)
    raw_part = jax.random.uniform(jax.random.fold_in(key, 34), (slot_total, W, W), jnp.float32, -1.0, 1.0) * (1.5 / W)
    symmetric = 0.5 * (raw_part + jnp.swapaxes(raw_part, 1, 2))
    gains = jax.random.uniform(jax.random.fold_in(key, 35), (slot_total, W), jnp.float32, 1.6, 3.2)
    diag_part = symmetric + jnp.eye(W, dtype=jnp.float32)[None] * gains[:, :, None]
    return jnp.where(on_diag, diag_part, off_part).astype(jnp.float32)


def setup_inputs(seed: int = 0) -> dict:
    seeds = jax.random.split(jax.random.key(seed), 3)
    blocks = draw_blocks(jax.random.fold_in(seeds[2], 71), 0)
    block_map = draw_block_map(jax.random.fold_in(seeds[2], 71), 0)
    return {"blocks": blocks, "block_map": block_map}


HIGHEST_PRECISION = lax.Precision.HIGHEST

def factor_panel(blocks, block_map, column):
    rows_all = block_map[:, 0]
    cols_all = block_map[:, 1]
    diag_slot = jnp.argmax(((rows_all == column) & (cols_all == column)).astype(jnp.int32)).astype(jnp.int32)
    lower_factor = jnp.linalg.cholesky(blocks[diag_slot])
    in_column = (cols_all == column).astype(jnp.int32)
    members = jnp.argsort(1 - in_column, stable=True)[:PANEL_ROWS].astype(jnp.int32)
    panel_old = blocks[members]
    stacked = jnp.transpose(panel_old, (2, 0, 1)).reshape(W, PANEL_ROWS * W)
    solved = lax.linalg.triangular_solve(lower_factor, stacked, left_side=True, lower=True)
    solved = solved.reshape(W, PANEL_ROWS, W).transpose(1, 2, 0)
    panel_rows = rows_all[members]
    on_diag = (panel_rows == column)[:, None, None]
    factored = jnp.where(on_diag, lower_factor[None], solved)
    blocks = blocks.at[members].set(factored)
    position = jnp.full((BLOCK_ROWS,), -1, jnp.int32).at[panel_rows].set(jnp.arange(PANEL_ROWS, dtype=jnp.int32))
    row_pos = position[rows_all]
    col_pos = position[cols_all]
    usable = (row_pos >= 0) & (col_pos >= 0) & (rows_all > column) & (cols_all > column)
    targets = jnp.argsort(1 - usable.astype(jnp.int32), stable=True)[:PANEL_ROWS * (PANEL_ROWS - 1) // 2].astype(jnp.int32)
    groups = targets.reshape(PANEL_ROWS // 2, PANEL_ROWS - 1)

    def product(batch_ids):
        left_side = factored[jnp.maximum(row_pos[batch_ids], 0)]
        right_side = factored[jnp.maximum(col_pos[batch_ids], 0)]
        update = jnp.einsum('sab,scb->sac', left_side, right_side, precision=HIGHEST_PRECISION)
        return update * usable[batch_ids].astype(jnp.float32)[:, None, None]
    updates = lax.map(product, groups).reshape(-1, W, W)
    return blocks.at[targets].add(-updates)

def reference(blocks, block_map):
    blocks = factor_panel(blocks, block_map, 0)
    blocks = factor_panel(blocks, block_map, 1)
    return blocks
```

```python
import jax
import jax.numpy as jnp
from jax import lax
from jax.experimental import pallas as pl
from jax.experimental.pallas import tpu as pltpu
from jax.sharding import PartitionSpec as P

PR = 4
W = 256
H = 128
G = 8
CHUNKS = 16
RING = 4
ROWS = 16
CHILDREN = (85, 40969, 4097, 32857)
MESH = pl.DeviceIdType.MESH
HIGHEST = lax.Precision.HIGHEST
F32 = jnp.float32


def dot_nn(a, b):
    return lax.dot_general(a, b, (((1,), (0,)), ((), ())), precision=HIGHEST, preferred_element_type=F32)


def dot_nt(a, b):
    return lax.dot_general(a, b, (((1,), (1,)), ((), ())), precision=HIGHEST, preferred_element_type=F32)


def tree_sum(terms):
    terms = list(terms)
    while len(terms) > 1:
        terms = [terms[i] + terms[i + 1] if i + 1 < len(terms) else terms[i] for i in range(0, len(terms), 2)]
    return terms[0]


def eliminate(p, c_ref, u_ref, x_ref):
    lo = p * G
    lane = lax.broadcasted_iota(jnp.int32, (G, H), 1)
    sub = lax.broadcasted_iota(jnp.int32, (G, H), 0)
    rows = c_ref[lo : lo + G, :]
    cols = [jnp.broadcast_to(rows[:, lo + j : lo + j + 1], (G, H)) for j in range(G)]
    a = {(i, j): jnp.broadcast_to(cols[j][i : i + 1, :], (G, H)) for j in range(G) for i in range(j, G)}
    low, inv, x = {}, [None] * G, {}
    for j in range(G):
        inv[j] = lax.rsqrt(a[j, j])
        for i in range(j + 1, G):
            low[i, j] = a[i, j] * inv[j]
        for k in range(j + 1, G):
            for i in range(k, G):
                a[i, k] = a[i, k] - low[i, j] * low[k, j]
    for j in range(G):
        x[j, j] = inv[j]
        for i in range(j + 1, G):
            x[i, j] = -(inv[i] * tree_sum([low[i, k] * x[k, j] for k in range(j, i)]))
    in_block = (lane >= lo) & (lane < lo + G)
    rows_with_eye = jnp.where(in_block, (lane - lo == sub).astype(F32), rows)

    def column(entry, ids):
        out = jnp.zeros((G, H), F32)
        for i in ids:
            out = jnp.where(sub == i, entry(i), out)
        return out

    def row(v, k):
        return jnp.broadcast_to(v[k : k + 1, :], (G, H))

    weights = [column(lambda i: x[i, k], range(k, G)) for k in range(G)]
    weights_t = [column(lambda i: x[k, i], range(0, k + 1)) for k in range(G)]
    reduced = tree_sum([weights[k] * row(rows_with_eye, k) for k in range(G)])
    upper = tree_sum([weights[k] * row(rows, k) for k in range(G)])
    u_ref[lo : lo + G, :] = jnp.where(lane >= lo + sub, upper, 0.0)
    x_ref[lo : lo + G, :] = jnp.where(lane < lo + G, reduced, 0.0)
    solved = tree_sum([weights_t[k] * row(reduced, k) for k in range(G)])
    solved_rows = [row(solved, k) for k in range(G)]
    for m in range(p + 1, H // G):
        old = c_ref[m * G : (m + 1) * G, :]
        taken = [jnp.broadcast_to(old[:, lo + k : lo + k + 1], (G, H)) * solved_rows[k] for k in range(G)]
        c_ref[m * G : (m + 1) * G, :] = jnp.where(in_block, 0.0, old) - tree_sum(taken)


def factor_128(c_ref, u_ref, x_ref):
    for p in range(H // G):
        eliminate(p, c_ref, u_ref, x_ref)


def factor_256(src, low_ref, inv_ref, c_ref, u_ref, x_ref, g_ref):
    zero = jnp.zeros((H, H), F32)
    c_ref[...] = src[0:H, 0:H]
    factor_128(c_ref, u_ref, x_ref)
    x1 = x_ref[...]
    inv_ref[0:H, 0:H] = x1
    inv_ref[0:H, H:W] = zero
    low_ref[0:H, 0:H] = u_ref[...].T
    low_ref[0:H, H:W] = zero
    below = dot_nt(src[H:W, 0:H], x1)
    low_ref[H:W, 0:H] = below
    c_ref[...] = src[H:W, H:W] - dot_nt(below, below)
    g_ref[...] = dot_nn(below, x1)
    factor_128(c_ref, u_ref, x_ref)
    x2 = x_ref[...]
    inv_ref[H:W, H:W] = x2
    low_ref[H:W, H:W] = u_ref[...].T
    inv_ref[H:W, 0:H] = -dot_nn(x2, g_ref[...])


def send_kernel(
    blk, idt, buf, idb, ch,
    dsrc, dpiece, dfull, chv, c_ref, u_ref, x_ref, g_ref,
    rs, ps, ri, pi, s_src, s_piece, s_full, s_to0, s_ch,
    t_x, t_tree, t_ix, t_itree, t_to0, t_ito0, t_src, t_scat, t_dx, t_gath, t_first, t_ch,
):
    w = lax.axis_index("wide")
    n = lax.axis_index("narrow")
    x, core = w // 2, w % 2
    y, z = n // RING, n % RING
    partner = (x * 2 + 1 - core, n)
    barrier = pltpu.get_barrier_semaphore()

    def chunk(ref, slot, k):
        return ref.at[slot, k // 2, pl.ds(pl.multiple_of((k % 2) * H, H), H)]

    def remote(src, dst, send, recv, device):
        return pltpu.make_async_remote_copy(
            src_ref=src, dst_ref=dst, send_sem=send, recv_sem=recv, device_id=device, device_id_type=MESH
        )

    def wait_bytes(ref, sem):
        pltpu.make_async_copy(ref, ref, sem).wait()

    def signal(device):
        pl.semaphore_signal(barrier, inc=1, device_id=device, device_id_type=MESH)

    def at_x(dx):
        return (lax.rem(x + dx, RING) * 2 + 1, n)

    @pl.when(core == 0)
    def _():
        @pl.loop(0, RING * RING)
        def _(i):
            signal((x * 2 + 1, i))

        pl.semaphore_wait(barrier, 1)

        @pl.when(x == 0)
        def _():
            @pl.when(n < 2)
            def _():
                remote(blk.at[0], dsrc, t_src, s_src, partner).start()

            remote(idt, idb.at[4, 0], t_first.at[0], ri, partner).start()
            for k in range(CHUNKS // 2):
                remote(chunk_of_block(blk, k), chunk(buf, 4, k), t_first.at[1], rs.at[k], partner).start()

        wait_bytes(dfull.at[0], s_full.at[0])
        factor_256(dfull.at[0], chv.at[0], chv.at[1], c_ref, u_ref, x_ref, g_ref)
        wait_bytes(dfull.at[1], s_full.at[1])
        l10 = dot_nt(dfull[1], chv[1])
        chv[2] = l10
        wait_bytes(dfull.at[2], s_full.at[2])
        dfull[2] = dfull[2] - dot_nt(l10, l10)
        factor_256(dfull.at[2], chv.at[3], chv.at[4], c_ref, u_ref, x_ref, g_ref)
        remote(chv, ch, t_ch.at[0], s_ch, partner).start()
        own = pltpu.make_async_copy(chv, ch, t_ch.at[1])
        own.start()

        @pl.when(x == 0)
        def _():
            @pl.when(n < 2)
            def _():
                wait_bytes(dsrc, t_src)

            wait_bytes(idt, t_first.at[0])
            wait_bytes(buf.at[4, pl.ds(0, PR)], t_first.at[1])

        for h in range(2):
            @pl.when(n != 2 * x + 8 * h)
            def _():
                wait_bytes(idb.at[2 * h], s_to0.at[2 * h])
                wait_bytes(buf.at[2 * h], s_to0.at[2 * h + 1])

        wait_bytes(idb.at[4], s_to0.at[4])
        wait_bytes(buf.at[4], s_to0.at[5])
        wait_bytes(chv, t_ch.at[0])
        own.wait()

    @pl.when(core == 1)
    def _():
        signal(partner)
        for dx in range(1, RING):
            signal(at_x(dx))

        @pl.loop(0, RING * RING)
        def _(i):
            @pl.when(i != n)
            def _():
                signal((w, i))

        pl.semaphore_wait(barrier, 2 * RING * RING - 1 + RING - 1)

        def scatter(b, src):
            @pl.loop(0, RING * RING)
            def _(i):
                part = src.at[pl.ds(pl.multiple_of(i * ROWS, ROWS), ROWS)]

                @pl.when(i != n)
                def _():
                    remote(part, dpiece.at[b], t_scat.at[b], s_piece.at[b], (w, i)).start()

                @pl.when(i == n)
                def _():
                    pltpu.make_async_copy(part, dpiece.at[b], s_piece.at[b]).start()

        @pl.when(x == 0)
        def _():
            @pl.when(n == 1)
            def _():
                scatter(2, blk.at[0])

            @pl.when(n < 2)
            def _():
                wait_bytes(dsrc, s_src)

                @pl.when(n == 0)
                def _():
                    scatter(0, dsrc)

                @pl.when(n == 1)
                def _():
                    scatter(1, dsrc)

            pltpu.make_async_copy(idt, idb.at[4, 1], ri).start()
            for k in range(CHUNKS // 2, CHUNKS):
                pltpu.make_async_copy(chunk_of_block(blk, k - CHUNKS // 2), chunk(buf, 4, k), rs.at[k]).start()
            wait_bytes(idb.at[4], ri)
            for j, dx in enumerate((1, RING - 1)):
                remote(idb.at[4], idb.at[4], t_ix.at[j], ri, at_x(dx)).start()

            @pl.loop(0, CHUNKS)
            def _(k):
                wait_bytes(chunk(buf, 4, k), rs.at[k])
                for j, dx in enumerate((1, RING - 1)):
                    remote(chunk(buf, 4, k), chunk(buf, 4, k), t_x.at[j], rs.at[k], at_x(dx)).start()

        for b in range(3):
            wait_bytes(dpiece.at[b], s_piece.at[b])

            @pl.when(x == 0)
            def _():
                for dx in range(1, RING):
                    remote(dpiece.at[b], dpiece.at[b], t_dx.at[b], s_piece.at[b], at_x(dx)).start()

            mine = pl.ds(pl.multiple_of(n * ROWS, ROWS), ROWS)

            @pl.loop(0, RING * RING)
            def _(i):
                remote(dpiece.at[b], dfull.at[b, mine], t_gath.at[b], s_full.at[b], (x * 2, i)).start()

        y_rel = lax.rem(y - x // 2 + RING, RING)
        z_rel = lax.rem(z - 2 * (x % 2) + RING, RING)
        steps = ((1, 0), (RING - 1, 0), (0, 1), (0, RING - 1))
        near = [(w, lax.rem(y + dy, RING) * RING + lax.rem(z + dz, RING)) for dy, dz in steps]
        sources, sends = [], []
        for g in range(4):
            h, q = g // 2, g % 2
            y_own = lax.rem(y_rel + 2 * h, RING)
            z_own = z_rel if q == 0 else lax.rem(1 - z_rel + RING, RING)
            index = y_own * RING + z_own
            flags = [(jnp.int32(mask) >> index) & 1 for mask in CHILDREN]
            if q == 1:
                flags[2], flags[3] = flags[3], flags[2]
            sources.append(index == 0)
            sends.append(flags)

        def pass_on(part, row_recv, row_from_x, tree_recv, x_send, tree_send, to0, to0_send, to0_row, x_odd):
            @pl.when(x != 0)
            def _():
                wait_bytes(part(4), row_recv)

                @pl.when(x == 1 + 2 * x_odd)
                def _():
                    remote(part(4), part(4), x_send, row_recv, (5, n)).start()

            remote(part(4), part(4), to0_send(4), to0_row, partner).start()
            for g in range(4):
                @pl.when(sources[g])
                def _():
                    for d in range(4):
                        remote(part(4), part(g), tree_send(g, d), tree_recv(g), near[d]).start()

                @pl.when(jnp.logical_not(sources[g]))
                def _():
                    wait_bytes(part(g), tree_recv(g))
                    for d in range(4):
                        @pl.when(sends[g][d] == 1)
                        def _():
                            remote(part(g), part(g), tree_send(g, d), tree_recv(g), near[d]).start()

                    if g % 2 == 0:
                        remote(part(g), part(g), to0_send(g), to0(g), partner).start()

        pass_on(
            lambda g: idb.at[g], ri, None, lambda g: pi.at[g], t_ix.at[0], lambda g, d: t_itree.at[g, d],
            lambda g: s_to0.at[g], lambda g: t_ito0.at[g], s_to0.at[4], 0,
        )

        @pl.loop(0, CHUNKS)
        def _(k):
            pass_on(
                lambda g: chunk(buf, g, k), rs.at[k], None, lambda g: ps.at[g, k], t_x.at[0],
                lambda g, d: t_tree.at[g, d], lambda g: s_to0.at[g + 1], lambda g: t_to0.at[g], s_to0.at[5], k % 2,
            )

        @pl.when(x == 0)
        def _():
            for j in range(2):
                wait_bytes(idb.at[4], t_ix.at[j])
                wait_bytes(buf.at[4], t_x.at[j])
            for b in range(3):
                for dx in range(1, RING):
                    wait_bytes(dpiece.at[b], t_dx.at[b])

            @pl.when(n == 0)
            def _():
                wait_bytes(dfull.at[0, pl.ds(0, W - ROWS)], t_scat.at[0])

            @pl.when(n == 1)
            def _():
                for b in (1, 2):
                    wait_bytes(dfull.at[b, pl.ds(0, W - ROWS)], t_scat.at[b])

        @pl.when(x == 1)
        def _():
            wait_bytes(idb.at[4], t_ix.at[0])

        @pl.when(x % 2 == 1)
        def _():
            wait_bytes(buf.at[4, pl.ds(0, PR)], t_x.at[0])

        for b in range(3):
            wait_bytes(dfull.at[b], t_gath.at[b])
        for g in range(4):
            for d in range(4):
                @pl.when(sources[g] | (sends[g][d] == 1))
                def _():
                    wait_bytes(idb.at[g], t_itree.at[g, d])
                    wait_bytes(buf.at[g], t_tree.at[g, d])
            if g % 2 == 0:
                @pl.when(jnp.logical_not(sources[g]))
                def _():
                    wait_bytes(idb.at[g], t_ito0.at[g])
                    wait_bytes(buf.at[g], t_to0.at[g])
        wait_bytes(idb.at[4], t_ito0.at[4])
        wait_bytes(buf.at[4], t_to0.at[4])
        wait_bytes(ch, s_ch)


def chunk_of_block(blk, k):
    return blk.at[k // 2, pl.ds((k % 2) * H, H)]


def split(a):
    high = a.astype(jnp.bfloat16)
    return high, (a - high.astype(F32)).astype(jnp.bfloat16)


def local_kernel(
    bmap, idb, blk, buf, ch, out,
    vb, pan, chv, low_r, low_c, row3, col3, g_ref, s_in, s_out, s_pan, s_ch,
):
    w = lax.axis_index("wide")
    n = lax.axis_index("narrow")
    x, core = w // 2, w % 2
    slots = blk.shape[0]
    piece = [jnp.where(n == w + 8 * h, 4, 2 * h + core) for h in range(2)]
    copies = [
        pltpu.make_async_copy(ch, chv, s_ch),
        pltpu.make_async_copy(buf.at[4], pan.at[0], s_pan.at[0]),
        pltpu.make_async_copy(buf.at[piece[0]], pan.at[1], s_pan.at[1]),
        pltpu.make_async_copy(buf.at[piece[1]], pan.at[2], s_pan.at[2]),
    ]
    for copy in copies:
        copy.start()

    @pl.loop(0, slots)
    def _(s):
        pltpu.make_async_copy(blk.at[s], vb.at[s], s_in.at[s]).start()

    for copy in copies:
        copy.wait()

    def find(slot, column, block_row):
        found = jnp.int32(-1)
        for i in range(PR):
            found = jnp.where(idb[slot, column, i, 0] == block_row, i, found)
        return found

    def store_row(i, value):
        low_r[i] = value
        high, rest = split(value)
        row3[i, :, 0:W] = high
        row3[i, :, W : 2 * W] = high
        row3[i, :, 2 * W : 3 * W] = rest

    def store_col(j, value):
        high, rest = split(value)
        col3[j, 0:W, :] = high
        col3[j, W : 2 * W, :] = rest
        col3[j, 2 * W : 3 * W, :] = high

    @pl.loop(0, PR)
    def _(i):
        store_row(i, dot_nt(pan[0, i], chv[1]))

    @pl.loop(0, 2 * PR)
    def _(j):
        value = dot_nt(chv[1], pan[1 + j // PR, j % PR])
        low_c[j] = value
        store_col(j, value)

    g_ref[...] = dot_nn(chv[4], chv[2])

    @pl.loop(0, PR)
    def _(i):
        from_first = find(4, 0, idb[4, 1, i, 0])
        pan[0, i] = dot_nt(pan[0, PR + i], chv[4])

        @pl.when((from_first >= 0) & (idb[4, 1, i, 0] > 0))
        def _():
            pan[0, i] = pan[0, i] - dot_nt(low_r[jnp.maximum(from_first, 0)], g_ref[...])

        store_row(PR + i, pan[0, i])

    @pl.loop(0, 2 * PR)
    def _(j):
        h, i = j // PR, j % PR
        slot = jnp.where(h == 0, piece[0], piece[1])
        block_row = idb[slot, 1, i, 0]
        from_first = find(slot, 0, block_row)
        pan[1 + h, i] = dot_nt(chv[4], pan[1 + h, PR + i])

        @pl.when((from_first >= 0) & (block_row > 0))
        def _():
            pan[1 + h, i] = pan[1 + h, i] - dot_nn(g_ref[...], low_c[h * PR + jnp.maximum(from_first, 0)])

        store_col(2 * PR + j, pan[1 + h, i])

    @pl.loop(0, slots)
    def _(s):
        r, c = bmap[s, 0], bmap[s, 1]
        h = (c % 16) // 8
        slot = jnp.where(h == 0, piece[0], piece[1])
        pltpu.make_async_copy(blk.at[s], vb.at[s], s_in.at[s]).wait()
        for column in range(2):
            i, j = find(4, column, r), find(slot, column, c)

            @pl.when((r > column) & (c > column) & (i >= 0) & (j >= 0))
            def _():
                vb[s] = vb[s] - jnp.dot(
                    row3[column * PR + jnp.maximum(i, 0)],
                    col3[column * 2 * PR + h * PR + jnp.maximum(j, 0)],
                    preferred_element_type=F32,
                )

            @pl.when((c == column) & (i >= 0))
            def _():
                vb[s] = low_r[column * PR + jnp.maximum(i, 0)]

                @pl.when(r == column)
                def _():
                    vb[s] = chv[3 * column]

        pltpu.make_async_copy(vb.at[s], out.at[s], s_out).start()

    pltpu.make_async_copy(vb, out, s_out).wait()


def on_device(blocks, block_map):
    ids = jnp.broadcast_to(jnp.pad(block_map[:PR, 0], (0, G - PR))[:, None], (G, H))
    anywhere = pl.BlockSpec(memory_space=pl.ANY)
    dma = pltpu.SemaphoreType.DMA
    vmem = pltpu.VMEM
    buf, idb, ch = pl.pallas_call(
        send_kernel,
        out_shape=[
            jax.ShapeDtypeStruct((5, 2 * PR, W, W), F32),
            jax.ShapeDtypeStruct((5, 2, G, H), jnp.int32),
            jax.ShapeDtypeStruct((5, W, W), F32),
        ],
        in_specs=[anywhere, anywhere],
        out_specs=[anywhere, anywhere, anywhere],
        scratch_shapes=[
            vmem((W, W), F32), vmem((3, ROWS, W), F32), vmem((3, W, W), F32), vmem((5, W, W), F32),
            vmem((H, H), F32), vmem((H, H), F32), vmem((H, H), F32), vmem((H, H), F32),
            dma((CHUNKS,)), dma((4, CHUNKS)), dma, dma((4,)), dma, dma((3,)), dma((3,)), dma((6,)), dma,
            dma((2,)), dma((4, 4)), dma((2,)), dma((4, 4)), dma((5,)), dma((5,)), dma, dma((3,)), dma((3,)), dma((3,)),
            dma((2,)), dma((2,)),
        ],
        compiler_params=pltpu.CompilerParams(collective_id=0, has_side_effects=True, vmem_limit_bytes=16 * 2**20),
    )(blocks, ids)
    slots = blocks.shape[0]
    return pl.pallas_call(
        local_kernel,
        out_shape=jax.ShapeDtypeStruct(blocks.shape, F32),
        in_specs=[
            pl.BlockSpec(memory_space=pltpu.SMEM), pl.BlockSpec(memory_space=pltpu.SMEM), anywhere, anywhere, anywhere,
        ],
        out_specs=anywhere,
        scratch_shapes=[
            vmem((slots, W, W), F32), vmem((3, 2 * PR, W, W), F32), vmem((5, W, W), F32),
            vmem((2 * PR, W, W), F32), vmem((2 * PR, W, W), F32),
            vmem((2 * PR, W, 3 * W), jnp.bfloat16), vmem((4 * PR, 3 * W, W), jnp.bfloat16), vmem((W, W), F32),
            dma((slots,)), dma, dma((3,)), dma,
        ],
        compiler_params=pltpu.CompilerParams(vmem_limit_bytes=44 * 2**20),
    )(block_map, idb, blocks, buf, ch)


def solution(mesh):
    return jax.shard_map(
        on_device,
        mesh=mesh,
        in_specs=(P(("wide", "narrow"), None, None), P(("wide", "narrow"), None)),
        out_specs=P(("wide", "narrow"), None, None),
        check_vma=False,
    )
```

```python
import jax
import jax.numpy as jnp
from jax import lax
from jax.experimental import pallas as pl
from jax.experimental.pallas import tpu as pltpu
from jax.sharding import PartitionSpec as P

PR = 4
W = 256
H = 128
G = 8
CHUNKS = 32
PARTS = CHUNKS // (2 * PR)
PART = W // PARTS
RING = 4
ROWS = 16
CHILDREN = (85, 40969, 4097, 32857)
DEPTH = (23130, 60356, 1056)
SKEW = 4
MESH = pl.DeviceIdType.MESH
HIGHEST = lax.Precision.HIGHEST
F32 = jnp.float32


def dot_nn(a, b):
    return lax.dot_general(a, b, (((1,), (0,)), ((), ())), precision=HIGHEST, preferred_element_type=F32)


def dot_nt(a, b):
    return lax.dot_general(a, b, (((1,), (1,)), ((), ())), precision=HIGHEST, preferred_element_type=F32)


def tree_sum(terms):
    terms = list(terms)
    while len(terms) > 1:
        terms = [terms[i] + terms[i + 1] if i + 1 < len(terms) else terms[i] for i in range(0, len(terms), 2)]
    return terms[0]


def eliminate(p, c_ref, u_ref, x_ref):
    lo = p * G
    lane = lax.broadcasted_iota(jnp.int32, (G, H), 1)
    sub = lax.broadcasted_iota(jnp.int32, (G, H), 0)
    rows = c_ref[lo : lo + G, :]
    cols = [jnp.broadcast_to(rows[:, lo + j : lo + j + 1], (G, H)) for j in range(G)]
    a = {(i, j): jnp.broadcast_to(cols[j][i : i + 1, :], (G, H)) for j in range(G) for i in range(j, G)}
    low, inv, x = {}, [None] * G, {}
    for j in range(G):
        inv[j] = lax.rsqrt(a[j, j])
        for i in range(j + 1, G):
            low[i, j] = a[i, j] * inv[j]
        for k in range(j + 1, G):
            for i in range(k, G):
                a[i, k] = a[i, k] - low[i, j] * low[k, j]
    for j in range(G):
        x[j, j] = inv[j]
        for i in range(j + 1, G):
            x[i, j] = -(inv[i] * tree_sum([low[i, k] * x[k, j] for k in range(j, i)]))
    in_block = (lane >= lo) & (lane < lo + G)
    rows_with_eye = jnp.where(in_block, (lane - lo == sub).astype(F32), rows)

    def column(entry, ids):
        out = jnp.zeros((G, H), F32)
        for i in ids:
            out = jnp.where(sub == i, entry(i), out)
        return out

    def row(v, k):
        return jnp.broadcast_to(v[k : k + 1, :], (G, H))

    weights = [column(lambda i: x[i, k], range(k, G)) for k in range(G)]
    weights_t = [column(lambda i: x[k, i], range(0, k + 1)) for k in range(G)]
    reduced = tree_sum([weights[k] * row(rows_with_eye, k) for k in range(G)])
    upper = tree_sum([weights[k] * row(rows, k) for k in range(G)])
    u_ref[lo : lo + G, :] = jnp.where(lane >= lo + sub, upper, 0.0)
    x_ref[lo : lo + G, :] = jnp.where(lane < lo + G, reduced, 0.0)
    solved = tree_sum([weights_t[k] * row(reduced, k) for k in range(G)])
    solved_rows = [row(solved, k) for k in range(G)]
    for m in range(p + 1, H // G):
        old = c_ref[m * G : (m + 1) * G, :]
        taken = [jnp.broadcast_to(old[:, lo + k : lo + k + 1], (G, H)) * solved_rows[k] for k in range(G)]
        c_ref[m * G : (m + 1) * G, :] = jnp.where(in_block, 0.0, old) - tree_sum(taken)


def factor_128(c_ref, u_ref, x_ref):
    for p in range(H // G):
        eliminate(p, c_ref, u_ref, x_ref)


def factor_256(src, low_ref, inv_ref, c_ref, u_ref, x_ref, g_ref):
    zero = jnp.zeros((H, H), F32)
    c_ref[...] = src[0:H, 0:H]
    factor_128(c_ref, u_ref, x_ref)
    x1 = x_ref[...]
    inv_ref[0:H, 0:H] = x1
    inv_ref[0:H, H:W] = zero
    low_ref[0:H, 0:H] = u_ref[...].T
    low_ref[0:H, H:W] = zero
    below = dot_nt(src[H:W, 0:H], x1)
    low_ref[H:W, 0:H] = below
    c_ref[...] = src[H:W, H:W] - dot_nt(below, below)
    g_ref[...] = dot_nn(below, x1)
    factor_128(c_ref, u_ref, x_ref)
    x2 = x_ref[...]
    inv_ref[H:W, H:W] = x2
    low_ref[H:W, H:W] = u_ref[...].T
    inv_ref[H:W, 0:H] = -dot_nn(x2, g_ref[...])


def send_kernel(
    blk, idt, buf, idb, ch,
    dsrc, dpiece, held, dfull, chv, c_ref, u_ref, x_ref, g_ref,
    rs, ps, ri, pi, s_src, s_piece, s_full, s_to0, s_ch,
    t_x, t_tree, t_ix, t_itree, t_to0, t_ito0, t_src, t_scat, t_dx, t_gath, t_first, t_ch,
):
    w = lax.axis_index("wide")
    n = lax.axis_index("narrow")
    x, core = w // 2, w % 2
    y, z = n // RING, n % RING
    partner = (x * 2 + 1 - core, n)
    barrier = pltpu.get_barrier_semaphore()

    def chunk(ref, slot, k):
        return ref.at[slot, k // PARTS, pl.ds(pl.multiple_of((k % PARTS) * PART, PART), PART)]

    def remote(src, dst, send, recv, device):
        return pltpu.make_async_remote_copy(
            src_ref=src, dst_ref=dst, send_sem=send, recv_sem=recv, device_id=device, device_id_type=MESH
        )

    def wait_bytes(ref, sem):
        pltpu.make_async_copy(ref, ref, sem).wait()

    def signal(device):
        pl.semaphore_signal(barrier, inc=1, device_id=device, device_id_type=MESH)

    def at_x(dx):
        return (lax.rem(x + dx, RING) * 2 + 1, n)

    @pl.when(core == 0)
    def _():
        @pl.loop(0, RING * RING)
        def _(i):
            signal((x * 2 + 1, i))

        pl.semaphore_wait(barrier, 1)

        @pl.when(x == 0)
        def _():
            @pl.when(n < 2)
            def _():
                remote(blk.at[0], dsrc, t_src, s_src, partner).start()

            remote(idt, idb.at[4, 0], t_first.at[0], ri, partner).start()
            for k in range(CHUNKS // 2):
                remote(chunk_of_block(blk, k), chunk(buf, 4, k), t_first.at[1], rs.at[k], partner).start()

        wait_bytes(dfull.at[0], s_full.at[0])
        factor_256(dfull.at[0], chv.at[0], chv.at[1], c_ref, u_ref, x_ref, g_ref)
        wait_bytes(dfull.at[1], s_full.at[1])
        l10 = dot_nt(dfull[1], chv[1])
        chv[2] = l10
        wait_bytes(dfull.at[2], s_full.at[2])
        dfull[2] = dfull[2] - dot_nt(l10, l10)
        factor_256(dfull.at[2], chv.at[3], chv.at[4], c_ref, u_ref, x_ref, g_ref)
        remote(chv, ch, t_ch.at[0], s_ch, partner).start()
        own = pltpu.make_async_copy(chv, ch, t_ch.at[1])
        own.start()

        @pl.when(x == 0)
        def _():
            @pl.when(n < 2)
            def _():
                wait_bytes(dsrc, t_src)

            wait_bytes(idt, t_first.at[0])
            wait_bytes(buf.at[4, pl.ds(0, PR)], t_first.at[1])

        for h in range(2):
            @pl.when(n != 2 * x + 8 * h)
            def _():
                wait_bytes(idb.at[2 * h], s_to0.at[2 * h])
                wait_bytes(buf.at[2 * h], s_to0.at[2 * h + 1])

        wait_bytes(idb.at[4], s_to0.at[4])
        wait_bytes(buf.at[4], s_to0.at[5])
        wait_bytes(chv, t_ch.at[0])
        own.wait()

    @pl.when(core == 1)
    def _():
        signal(partner)
        for dx in range(1, RING):
            signal(at_x(dx))

        @pl.loop(0, RING * RING)
        def _(i):
            @pl.when(i != n)
            def _():
                signal((w, i))

        pl.semaphore_wait(barrier, 2 * RING * RING - 1 + RING - 1)

        def scatter(b, src):
            @pl.loop(0, RING * RING)
            def _(i):
                part = src.at[pl.ds(pl.multiple_of(i * ROWS, ROWS), ROWS)]

                @pl.when(i != n)
                def _():
                    remote(part, dpiece.at[b], t_scat.at[b], s_piece.at[b], (w, i)).start()

                @pl.when(i == n)
                def _():
                    pltpu.make_async_copy(part, dpiece.at[b], s_piece.at[b]).start()

        @pl.when(x == 0)
        def _():
            @pl.when(n == 1)
            def _():
                scatter(2, blk.at[0])

            @pl.when(n < 2)
            def _():
                wait_bytes(dsrc, s_src)

                @pl.when(n == 0)
                def _():
                    scatter(0, dsrc)

                @pl.when(n == 1)
                def _():
                    scatter(1, dsrc)

            pltpu.make_async_copy(idt, idb.at[4, 1], ri).start()
            pltpu.make_async_copy(blk.at[pl.ds(0, PR)], held, t_first.at[0]).start()
            wait_bytes(held, t_first.at[0])
            for k in range(CHUNKS // 2, CHUNKS):
                pltpu.make_async_copy(chunk_of_block(held, k - CHUNKS // 2), chunk(buf, 4, k), rs.at[k]).start()

        for b in range(3):
            wait_bytes(dpiece.at[b], s_piece.at[b])

            @pl.when(x == 0)
            def _():
                for dx in range(1, RING):
                    remote(dpiece.at[b], dpiece.at[b], t_dx.at[b], s_piece.at[b], at_x(dx)).start()

            mine = pl.ds(pl.multiple_of(n * ROWS, ROWS), ROWS)

            @pl.loop(0, RING * RING)
            def _(i):
                remote(dpiece.at[b], dfull.at[b, mine], t_gath.at[b], s_full.at[b], (x * 2, i)).start()

        y_rel = lax.rem(y - x // 2 + RING, RING)
        z_rel = lax.rem(z - 2 * (x % 2) + RING, RING)
        steps = ((1, 0), (RING - 1, 0), (0, 1), (0, RING - 1))
        near = [(w, lax.rem(y + dy, RING) * RING + lax.rem(z + dz, RING)) for dy, dz in steps]
        sources, sends, depths = [], [], []
        for g in range(4):
            h, q = g // 2, g % 2
            y_own = lax.rem(y_rel + 2 * h, RING)
            z_own = z_rel if q == 0 else lax.rem(1 - z_rel + RING, RING)
            index = y_own * RING + z_own
            flags = [(jnp.int32(mask) >> index) & 1 for mask in CHILDREN]
            if q == 1:
                flags[2], flags[3] = flags[3], flags[2]
            depths.append(sum(((jnp.int32(mask) >> index) & 1) << b for b, mask in enumerate(DEPTH)))
            sources.append(index == 0)
            sends.append(flags)

        def pass_row(part, recv, x_send, send, to0, to0_send, tree_recv, x_odd):
            wait_bytes(part(4), recv)

            @pl.when(x == 0)
            def _():
                for j, dx in enumerate((1, RING - 1)):
                    remote(part(4), part(4), x_send.at[j], recv, at_x(dx)).start()

            @pl.when(x == 1 + 2 * x_odd)
            def _():
                remote(part(4), part(4), x_send.at[0], recv, (5, n)).start()

            for g in range(4):
                @pl.when(sources[g])
                def _():
                    for d in range(4):
                        remote(part(4), part(g), send(g, d), tree_recv(g), near[d]).start()

            remote(part(4), part(4), to0_send(4), to0, partner).start()

        def pass_piece(g, part, recv, send, to0, to0_send):
            wait_bytes(part(g), recv)
            for d in range(4):
                @pl.when(sends[g][d] == 1)
                def _():
                    remote(part(g), part(g), send(g, d), recv, near[d]).start()

            if g % 2 == 0:
                remote(part(g), part(g), to0_send(g), to0(g), partner).start()

        @pl.loop(0, CHUNKS + 4 * SKEW)
        def _(t):
            @pl.when(t == 0)
            def _():
                pass_row(
                    lambda g: idb.at[g], ri, t_ix, lambda g, d: t_itree.at[g, d], s_to0.at[4],
                    lambda g: t_ito0.at[g], lambda g: pi.at[g], 0,
                )

            @pl.when(t < CHUNKS)
            def _():
                k = jnp.minimum(t, CHUNKS - 1)
                pass_row(
                    lambda g: chunk(buf, g, k), rs.at[k], t_x, lambda g, d: t_tree.at[g, d], s_to0.at[5],
                    lambda g: t_to0.at[g], lambda g: ps.at[g, k], k % 2,
                )

            for g in range(4):
                late = t - SKEW * depths[g]

                @pl.when(jnp.logical_not(sources[g]) & (late == 0))
                def _():
                    pass_piece(
                        g, lambda g: idb.at[g], pi.at[g], lambda g, d: t_itree.at[g, d], lambda g: s_to0.at[g],
                        lambda g: t_ito0.at[g],
                    )

                @pl.when(jnp.logical_not(sources[g]) & (late >= 0) & (late < CHUNKS))
                def _():
                    k = jnp.minimum(jnp.maximum(late, 0), CHUNKS - 1)
                    pass_piece(
                        g, lambda g: chunk(buf, g, k), ps.at[g, k], lambda g, d: t_tree.at[g, d],
                        lambda g: s_to0.at[g + 1], lambda g: t_to0.at[g],
                    )

        @pl.when(x == 0)
        def _():
            for j in range(2):
                wait_bytes(idb.at[4], t_ix.at[j])
                wait_bytes(buf.at[4], t_x.at[j])
            for b in range(3):
                for dx in range(1, RING):
                    wait_bytes(dpiece.at[b], t_dx.at[b])

            @pl.when(n == 0)
            def _():
                wait_bytes(dfull.at[0, pl.ds(0, W - ROWS)], t_scat.at[0])

            @pl.when(n == 1)
            def _():
                for b in (1, 2):
                    wait_bytes(dfull.at[b, pl.ds(0, W - ROWS)], t_scat.at[b])

        @pl.when(x == 1)
        def _():
            wait_bytes(idb.at[4], t_ix.at[0])

        @pl.when(x % 2 == 1)
        def _():
            wait_bytes(buf.at[4, pl.ds(0, PR)], t_x.at[0])

        for b in range(3):
            wait_bytes(dfull.at[b], t_gath.at[b])
        for g in range(4):
            for d in range(4):
                @pl.when(sources[g] | (sends[g][d] == 1))
                def _():
                    wait_bytes(idb.at[g], t_itree.at[g, d])
                    wait_bytes(buf.at[g], t_tree.at[g, d])
            if g % 2 == 0:
                @pl.when(jnp.logical_not(sources[g]))
                def _():
                    wait_bytes(idb.at[g], t_ito0.at[g])
                    wait_bytes(buf.at[g], t_to0.at[g])
        wait_bytes(idb.at[4], t_ito0.at[4])
        wait_bytes(buf.at[4], t_to0.at[4])
        wait_bytes(ch, s_ch)


def chunk_of_block(blk, k):
    return blk.at[k // PARTS, pl.ds((k % PARTS) * PART, PART)]


def split(a):
    high = a.astype(jnp.bfloat16)
    rest = a - high.astype(F32)
    middle = rest.astype(jnp.bfloat16)
    return high, middle, (rest - middle.astype(F32)).astype(jnp.bfloat16)


def left_terms(h, m, low):
    return [h, h, m, h, m, low]


def right_terms(h, m, low):
    return [h, m, h, low, m, h]


def stacked_dot(left, right):
    return lax.dot_general(
        jnp.concatenate(left, axis=1), jnp.concatenate(right, axis=1),
        (((1,), (1,)), ((), ())), preferred_element_type=F32,
    )


def local_kernel(
    bmap, idb, blk, buf, ch, out,
    vb, pan, chv, parts, inv_parts, prod, where_to, s_in, s_out, s_pan, s_ch,
):
    w = lax.axis_index("wide")
    n = lax.axis_index("narrow")
    core = w % 2
    slots = blk.shape[0]
    slot_of = [jnp.int32(4)] + [jnp.where(n == w + 8 * h, 4, 2 * h + core) for h in range(2)]
    copies = [pltpu.make_async_copy(ch, chv, s_ch)]
    for column in range(2):
        for q in range(3):
            copies.append(
                pltpu.make_async_copy(
                    buf.at[slot_of[q], pl.ds(column * PR, PR)], pan.at[column, pl.ds(q * PR, PR)], s_pan.at[column, q]
                )
            )
    for copy in copies:
        copy.start()

    def find(slot, column, block_row):
        found = jnp.int32(-1)
        for i in range(PR):
            found = jnp.where(idb[slot, column, 0, i] == block_row, i, found)
        return found

    @pl.loop(0, slots)
    def _(s):
        r, c = bmap[0, s], bmap[1, s]
        h = (c % 16) // 8
        i, j = find(4, 1, r), find(jnp.where(h == 0, slot_of[1], slot_of[2]), 1, c)
        code = jnp.where((c > 1) & (i >= 0) & (j >= 0), i + PR * (j + PR * h), -1)
        code = jnp.where(c == 0, 32 + find(4, 0, r), jnp.where(c == 1, 32 + i, code))
        where_to[s] = code

        @pl.when(code < 32)
        def _():
            pltpu.make_async_copy(blk.at[s], vb.at[s], s_in.at[s]).start()

    for copy in copies:
        copy.wait()

    first_inv = split(chv[1])
    for k in range(3):
        inv_parts[:, k * W : (k + 1) * W] = first_inv[k]
    second_inv = split(chv[4])
    coupling = split(-dot_nn(chv[4], chv[2]))
    for k in range(3):
        inv_parts[:, (3 + k) * W : (4 + k) * W] = second_inv[k]
        inv_parts[:, (6 + k) * W : (7 + k) * W] = coupling[k]

    def inverse(t):
        return [inv_parts[:, (3 * t + k) * W : (3 * t + k + 1) * W] for k in range(3)]

    @pl.loop(0, 3 * PR // 2)
    def _(b):
        old = pan[0, pl.ds(2 * b, 2)].reshape(2 * W, W)
        value = stacked_dot(left_terms(*split(old)), right_terms(*inverse(0)))
        pan[0, pl.ds(2 * b, 2)] = value.reshape(2, W, W)

    @pl.loop(0, slots)
    def _(s):
        @pl.when(where_to[s] < 0)
        def _():
            pltpu.make_async_copy(blk.at[s], vb.at[s], s_in.at[s]).wait()
            pltpu.make_async_copy(vb.at[s], out.at[s], s_out).start()

    @pl.loop(0, 3 * PR // 2)
    def _(b):
        q = b // 2
        slot = jnp.where(q == 0, slot_of[0], jnp.where(q == 1, slot_of[1], slot_of[2]))
        firsts = []
        for d in range(2):
            block_row = idb[slot, 1, 0, (2 * b + d) % PR]
            i = find(slot, 0, block_row)
            value = pan[0, q * PR + jnp.maximum(i, 0)]
            firsts.append(jnp.where((i >= 0) & (block_row > 0), value, 0.0))
        first = split(jnp.concatenate(firsts, axis=0))
        old = split(pan[1, pl.ds(2 * b, 2)].reshape(2 * W, W))
        value = stacked_dot(
            left_terms(*old) + left_terms(*first), right_terms(*inverse(1)) + right_terms(*inverse(2))
        )
        pan[1, pl.ds(2 * b, 2)] = value.reshape(2, W, W)
        second = split(value)
        for k, part in enumerate((first[0], first[1], second[0], second[1])):
            parts[pl.ds(2 * b, 2), :, k * W : (k + 1) * W] = part.reshape(2, W, W)

    def part(at, count, k):
        return parts[at, :, k * W : (k + 1) * W].reshape(count * W, W)

    @pl.loop(0, 2 * PR)
    def _(j):
        left = [part(pl.ds(0, PR), PR, k) for k in (0, 0, 1, 2, 2, 3)]
        right = [part(pl.ds(PR + j, 1), 1, k) for k in (0, 1, 0, 2, 3, 2)]
        prod[j] = stacked_dot(left, right).reshape(PR, W, W)

    @pl.loop(0, slots)
    def _(s):
        code = where_to[s]

        @pl.when((code >= 0) & (code < 32))
        def _():
            pltpu.make_async_copy(blk.at[s], vb.at[s], s_in.at[s]).wait()
            vb[s] = vb[s] - prod[jnp.maximum(code, 0) // PR, jnp.maximum(code, 0) % PR]

        @pl.when(code >= 32)
        def _():
            r, c = bmap[0, s], bmap[1, s]

            @pl.when(r == c)
            def _():
                vb[s] = chv[3 * c]

            @pl.when(r != c)
            def _():
                vb[s] = pan[c, code - 32]

        @pl.when(code >= 0)
        def _():
            pltpu.make_async_copy(vb.at[s], out.at[s], s_out).start()

    pltpu.make_async_copy(out, out, s_out).wait()


def on_device(blocks, block_map):
    ids = block_map.T
    anywhere = pl.BlockSpec(memory_space=pltpu.HBM)
    dma = pltpu.SemaphoreType.DMA
    vmem = pltpu.VMEM
    buf, idb, ch = pl.pallas_call(
        send_kernel,
        out_shape=[
            jax.ShapeDtypeStruct((5, 2 * PR, W, W), F32),
            jax.ShapeDtypeStruct((5, 2) + ids.shape, jnp.int32),
            jax.ShapeDtypeStruct((5, W, W), F32),
        ],
        in_specs=[anywhere, anywhere],
        out_specs=[anywhere, anywhere, anywhere],
        scratch_shapes=[
            vmem((W, W), F32), vmem((3, ROWS, W), F32), vmem((PR, W, W), F32), vmem((3, W, W), F32), vmem((5, W, W), F32),
            vmem((H, H), F32), vmem((H, H), F32), vmem((H, H), F32), vmem((H, H), F32),
            dma((CHUNKS,)), dma((4, CHUNKS)), dma, dma((4,)), dma, dma((3,)), dma((3,)), dma((6,)), dma,
            dma((2,)), dma((4, 4)), dma((2,)), dma((4, 4)), dma((5,)), dma((5,)), dma, dma((3,)), dma((3,)), dma((3,)),
            dma((2,)), dma((2,)),
        ],
        compiler_params=pltpu.CompilerParams(collective_id=0, has_side_effects=True, vmem_limit_bytes=60 * 2**20),
    )(blocks, ids)
    slots = blocks.shape[0]
    return pl.pallas_call(
        local_kernel,
        out_shape=jax.ShapeDtypeStruct(blocks.shape, F32),
        in_specs=[
            pl.BlockSpec(memory_space=pltpu.SMEM), pl.BlockSpec(memory_space=pltpu.SMEM), anywhere, anywhere, anywhere,
        ],
        out_specs=anywhere,
        scratch_shapes=[
            vmem((slots, W, W), F32), vmem((2, 3 * PR, W, W), F32), vmem((5, W, W), F32),
            vmem((3 * PR, W, 4 * W), jnp.bfloat16), vmem((W, 9 * W), jnp.bfloat16), vmem((2 * PR, PR, W, W), F32),
            pltpu.SMEM((slots,), jnp.int32),
            dma((slots,)), dma, dma((2, 3)), dma,
        ],
        compiler_params=pltpu.CompilerParams(vmem_limit_bytes=60 * 2**20),
    )(ids, idb, blocks, buf, ch)


def solution(mesh):
    return jax.shard_map(
        on_device,
        mesh=mesh,
        in_specs=(P(("wide", "narrow"), None, None), P(("wide", "narrow"), None)),
        out_specs=P(("wide", "narrow"), None, None),
        check_vma=False,
    )
```

```python
import jax
import jax.numpy as jnp
from jax import lax
from jax.experimental import pallas as pl
from jax.experimental.pallas import tpu as pltpu
from jax.sharding import PartitionSpec as P

PR = 4
W = 256
H = 128
G = 8
CHUNKS = 32
PARTS = CHUNKS // (2 * PR)
PART = W // PARTS
RING = 4
ROWS = 16
CHILDREN = (85, 40969, 4097, 32857)
DEPTH = (23130, 60356, 1056)
SKEW = 5
MESH = pl.DeviceIdType.MESH
HIGHEST = lax.Precision.HIGHEST
F32 = jnp.float32


def dot_nn(a, b):
    return lax.dot_general(a, b, (((1,), (0,)), ((), ())), precision=HIGHEST, preferred_element_type=F32)


def dot_nt(a, b):
    return lax.dot_general(a, b, (((1,), (1,)), ((), ())), precision=HIGHEST, preferred_element_type=F32)


def tree_sum(terms):
    terms = list(terms)
    while len(terms) > 1:
        terms = [terms[i] + terms[i + 1] if i + 1 < len(terms) else terms[i] for i in range(0, len(terms), 2)]
    return terms[0]


def eliminate(p, c_ref, u_ref, x_ref):
    lo = p * G
    lane = lax.broadcasted_iota(jnp.int32, (G, H), 1)
    sub = lax.broadcasted_iota(jnp.int32, (G, H), 0)
    rows = c_ref[lo : lo + G, :]
    cols = [jnp.broadcast_to(rows[:, lo + j : lo + j + 1], (G, H)) for j in range(G)]
    a = {(i, j): jnp.broadcast_to(cols[j][i : i + 1, :], (G, H)) for j in range(G) for i in range(j, G)}
    low, inv, x = {}, [None] * G, {}
    for j in range(G):
        inv[j] = lax.rsqrt(a[j, j])
        for i in range(j + 1, G):
            low[i, j] = a[i, j] * inv[j]
        for k in range(j + 1, G):
            for i in range(k, G):
                a[i, k] = a[i, k] - low[i, j] * low[k, j]
    for j in range(G):
        x[j, j] = inv[j]
        for i in range(j + 1, G):
            x[i, j] = -(inv[i] * tree_sum([low[i, k] * x[k, j] for k in range(j, i)]))
    in_block = (lane >= lo) & (lane < lo + G)
    rows_with_eye = jnp.where(in_block, (lane - lo == sub).astype(F32), rows)

    def column(entry, ids):
        out = jnp.zeros((G, H), F32)
        for i in ids:
            out = jnp.where(sub == i, entry(i), out)
        return out

    def row(v, k):
        return jnp.broadcast_to(v[k : k + 1, :], (G, H))

    weights = [column(lambda i: x[i, k], range(k, G)) for k in range(G)]
    weights_t = [column(lambda i: x[k, i], range(0, k + 1)) for k in range(G)]
    reduced = tree_sum([weights[k] * row(rows_with_eye, k) for k in range(G)])
    upper = tree_sum([weights[k] * row(rows, k) for k in range(G)])
    u_ref[lo : lo + G, :] = jnp.where(lane >= lo + sub, upper, 0.0)
    x_ref[lo : lo + G, :] = jnp.where(lane < lo + G, reduced, 0.0)
    solved = tree_sum([weights_t[k] * row(reduced, k) for k in range(G)])
    solved_rows = [row(solved, k) for k in range(G)]
    for m in range(p + 1, H // G):
        old = c_ref[m * G : (m + 1) * G, :]
        taken = [jnp.broadcast_to(old[:, lo + k : lo + k + 1], (G, H)) * solved_rows[k] for k in range(G)]
        c_ref[m * G : (m + 1) * G, :] = jnp.where(in_block, 0.0, old) - tree_sum(taken)


def factor_128(c_ref, u_ref, x_ref):
    for p in range(H // G):
        eliminate(p, c_ref, u_ref, x_ref)


def factor_256(src, low_ref, inv_ref, c_ref, u_ref, x_ref, g_ref):
    zero = jnp.zeros((H, H), F32)
    c_ref[...] = src[0:H, 0:H]
    factor_128(c_ref, u_ref, x_ref)
    x1 = x_ref[...]
    inv_ref[0:H, 0:H] = x1
    inv_ref[0:H, H:W] = zero
    low_ref[0:H, 0:H] = u_ref[...].T
    low_ref[0:H, H:W] = zero
    below = dot_nt(src[H:W, 0:H], x1)
    low_ref[H:W, 0:H] = below
    c_ref[...] = src[H:W, H:W] - dot_nt(below, below)
    g_ref[...] = dot_nn(below, x1)
    factor_128(c_ref, u_ref, x_ref)
    x2 = x_ref[...]
    inv_ref[H:W, H:W] = x2
    low_ref[H:W, H:W] = u_ref[...].T
    inv_ref[H:W, 0:H] = -dot_nn(x2, g_ref[...])


def send_kernel(
    blk, idt, buf, idb, ch,
    dsrc, dpiece, held, dfull, chv, c_ref, u_ref, x_ref, g_ref,
    rs, ps, ri, pi, s_src, s_piece, s_full, s_to0, s_ch,
    t_x, t_tree, t_ix, t_itree, t_to0, t_ito0, t_src, t_scat, t_dx, t_gath, t_first, t_ch,
):
    w = lax.axis_index("wide")
    n = lax.axis_index("narrow")
    x, core = w // 2, w % 2
    y, z = n // RING, n % RING
    partner = (x * 2 + 1 - core, n)
    barrier = pltpu.get_barrier_semaphore()

    def chunk(ref, slot, k):
        return ref.at[slot, k // PARTS, pl.ds(pl.multiple_of((k % PARTS) * PART, PART), PART)]

    def remote(src, dst, send, recv, device):
        return pltpu.make_async_remote_copy(
            src_ref=src, dst_ref=dst, send_sem=send, recv_sem=recv, device_id=device, device_id_type=MESH
        )

    def wait_bytes(ref, sem):
        pltpu.make_async_copy(ref, ref, sem).wait()

    def signal(device):
        pl.semaphore_signal(barrier, inc=1, device_id=device, device_id_type=MESH)

    def at_x(dx):
        return (lax.rem(x + dx, RING) * 2 + 1, n)

    @pl.when(core == 0)
    def _():
        signal(partner)
        for dx in range(1, RING):
            signal((lax.rem(x + dx, RING) * 2, n))

        @pl.loop(0, RING * RING)
        def _(i):
            @pl.when(i != n)
            def _():
                signal((w, i))

        pl.semaphore_wait(barrier, RING * RING + RING - 1)

        def scatter(b, src):
            @pl.loop(0, RING * RING)
            def _(i):
                part = src.at[pl.ds(pl.multiple_of(i * ROWS, ROWS), ROWS)]

                @pl.when(i != n)
                def _():
                    remote(part, dpiece.at[b], t_scat.at[b], s_piece.at[b], (w, i)).start()

                @pl.when(i == n)
                def _():
                    pltpu.make_async_copy(part, dpiece.at[b], s_piece.at[b]).start()

        @pl.when(x == 0)
        def _():
            @pl.when(n == 0)
            def _():
                scatter(0, blk.at[0])

            @pl.when(n == 1)
            def _():
                scatter(1, blk.at[0])

            remote(idt, idb.at[4, 0], t_first.at[0], ri, partner).start()
            for k in range(CHUNKS // 2):
                remote(chunk_of_block(blk, k), chunk(buf, 4, k), t_first.at[1], rs.at[k], partner).start()

            @pl.when(n == 1)
            def _():
                wait_bytes(dsrc, s_src)
                scatter(2, dsrc)

        mine = pl.ds(pl.multiple_of(n * ROWS, ROWS), ROWS)
        for b in range(3):
            wait_bytes(dpiece.at[b], s_piece.at[b])

            @pl.when(x == 0)
            def _():
                for dx in range(1, RING):
                    remote(dpiece.at[b], dpiece.at[b], t_dx.at[b], s_piece.at[b], (dx * 2, n)).start()

            @pl.loop(0, RING * RING)
            def _(i):
                @pl.when(i != n)
                def _():
                    remote(dpiece.at[b], dfull.at[b, mine], t_gath.at[b], s_full.at[b], (w, i)).start()

                @pl.when(i == n)
                def _():
                    pltpu.make_async_copy(dpiece.at[b], dfull.at[b, mine], s_full.at[b]).start()

        wait_bytes(dfull.at[0], s_full.at[0])
        factor_256(dfull.at[0], chv.at[0], chv.at[1], c_ref, u_ref, x_ref, g_ref)
        wait_bytes(dfull.at[1], s_full.at[1])
        l10 = dot_nt(dfull[1], chv[1])
        chv[2] = l10
        wait_bytes(dfull.at[2], s_full.at[2])
        dfull[2] = dfull[2] - dot_nt(l10, l10)
        factor_256(dfull.at[2], chv.at[3], chv.at[4], c_ref, u_ref, x_ref, g_ref)
        remote(chv, ch, t_ch.at[0], s_ch, partner).start()
        own = pltpu.make_async_copy(chv, ch, t_ch.at[1])
        own.start()

        @pl.when(x == 0)
        def _():
            for b in range(3):
                for dx in range(1, RING):
                    wait_bytes(dpiece.at[b], t_dx.at[b])

            @pl.when(n == 0)
            def _():
                wait_bytes(dfull.at[0, pl.ds(0, W - ROWS)], t_scat.at[0])

            @pl.when(n == 1)
            def _():
                for b in (1, 2):
                    wait_bytes(dfull.at[b, pl.ds(0, W - ROWS)], t_scat.at[b])

            wait_bytes(idt, t_first.at[0])
            wait_bytes(buf.at[4, pl.ds(0, PR)], t_first.at[1])

        for b in range(3):
            wait_bytes(dfull.at[b, pl.ds(0, W - ROWS)], t_gath.at[b])
        for h in range(2):
            @pl.when(n != 2 * x + 8 * h)
            def _():
                wait_bytes(idb.at[2 * h], s_to0.at[2 * h])
                wait_bytes(buf.at[2 * h], s_to0.at[2 * h + 1])

        wait_bytes(idb.at[4], s_to0.at[4])
        wait_bytes(buf.at[4], s_to0.at[5])
        wait_bytes(chv, t_ch.at[0])
        own.wait()

    @pl.when(core == 1)
    def _():
        steps = ((1, 0), (RING - 1, 0), (0, 1), (0, RING - 1))
        near = [(w, lax.rem(y + dy, RING) * RING + lax.rem(z + dz, RING)) for dy, dz in steps]
        signal(partner)
        for dx in range(1, RING):
            signal(at_x(dx))
        for device in near:
            signal(device)
        pl.semaphore_wait(barrier, 1 + RING - 1 + len(near))

        @pl.when(x == 0)
        def _():
            @pl.when(n == 1)
            def _():
                remote(blk.at[0], dsrc, t_src, s_src, partner).start()

            pltpu.make_async_copy(idt, idb.at[4, 1], ri).start()
            pltpu.make_async_copy(blk.at[pl.ds(0, PR)], held, t_first.at[0]).start()
            wait_bytes(held, t_first.at[0])
            for k in range(CHUNKS // 2, CHUNKS):
                pltpu.make_async_copy(chunk_of_block(held, k - CHUNKS // 2), chunk(buf, 4, k), rs.at[k]).start()

        y_rel = lax.rem(y - x // 2 + RING, RING)
        z_rel = lax.rem(z - 2 * (x % 2) + RING, RING)
        sources, sends, depths = [], [], []
        for g in range(4):
            h, q = g // 2, g % 2
            y_own = lax.rem(y_rel + 2 * h, RING)
            z_own = z_rel if q == 0 else lax.rem(1 - z_rel + RING, RING)
            index = y_own * RING + z_own
            flags = [(jnp.int32(mask) >> index) & 1 for mask in CHILDREN]
            if q == 1:
                flags[2], flags[3] = flags[3], flags[2]
            depths.append(sum(((jnp.int32(mask) >> index) & 1) << b for b, mask in enumerate(DEPTH)))
            sources.append(index == 0)
            sends.append(flags)

        out_any, out_g, out_slot, out_lag = [], [], [], []
        for d in range(4):
            here = [jnp.where(sources[g], 1, sends[g][d]) for g in range(4)]
            out_any.append(sum(here) > 0)
            out_g.append(sum(g * here[g] for g in range(4)))
            out_slot.append(sum(jnp.where(sources[g], 4, g) * here[g] for g in range(4)))
            out_lag.append(sum(SKEW * depths[g] * here[g] for g in range(4)))
        lags = [jnp.where(sources[g], CHUNKS + 4 * SKEW, SKEW * depths[g]) for g in range(4)]

        def pass_row(part, recv, x_send, x_odd):
            wait_bytes(part, recv)

            @pl.when(x == 0)
            def _():
                for j, dx in enumerate((1, RING - 1)):
                    remote(part, part, x_send.at[j], recv, at_x(dx)).start()

            @pl.when(x == 1 + 2 * x_odd)
            def _():
                remote(part, part, x_send.at[0], recv, (5, n)).start()

        def block_over(slot, k, send, recv):
            @pl.when(k % PARTS == PARTS - 1)
            def _():
                block = buf.at[slot, k // PARTS]
                remote(block, block, send, recv, partner).start()

        @pl.loop(0, CHUNKS + 4 * SKEW)
        def _(t):
            @pl.when(t < CHUNKS)
            def _():
                k = jnp.minimum(t, CHUNKS - 1)

                @pl.when(t == 0)
                def _():
                    pass_row(idb.at[4], ri, t_ix, 0)
                    remote(idb.at[4], idb.at[4], t_ito0.at[4], s_to0.at[4], partner).start()

                pass_row(chunk(buf, 4, k), rs.at[k], t_x, k % 2)

            for g in range(4):
                late = t - lags[g]

                @pl.when((late >= 0) & (late < CHUNKS))
                def _():
                    k = jnp.minimum(jnp.maximum(late, 0), CHUNKS - 1)
                    wait_bytes(chunk(buf, g, k), ps.at[g, k])

                    @pl.when(late == 0)
                    def _():
                        wait_bytes(idb.at[g], pi.at[g])
                        if g % 2 == 0:
                            remote(idb.at[g], idb.at[g], t_ito0.at[g], s_to0.at[g], partner).start()

            for d in range(4):
                late = t - out_lag[d]

                @pl.when(out_any[d] & (late >= 0) & (late < CHUNKS))
                def _():
                    k = jnp.minimum(jnp.maximum(late, 0), CHUNKS - 1)
                    g, slot = out_g[d], out_slot[d]

                    @pl.when(late == 0)
                    def _():
                        remote(idb.at[slot], idb.at[g], t_itree.at[d], pi.at[g], near[d]).start()

                    remote(chunk(buf, slot, k), chunk(buf, g, k), t_tree.at[d], ps.at[g, k], near[d]).start()

            @pl.when(t < CHUNKS)
            def _():
                block_over(4, jnp.minimum(t, CHUNKS - 1), t_to0.at[4], s_to0.at[5])

            for g in (0, 2):
                late = t - lags[g]

                @pl.when((late >= 0) & (late < CHUNKS))
                def _():
                    block_over(g, jnp.minimum(jnp.maximum(late, 0), CHUNKS - 1), t_to0.at[g], s_to0.at[g + 1])

        @pl.when(x == 0)
        def _():
            for j in range(2):
                wait_bytes(idb.at[4], t_ix.at[j])
                wait_bytes(buf.at[4], t_x.at[j])
            @pl.when(n == 1)
            def _():
                wait_bytes(dsrc, t_src)

        @pl.when(x == 1)
        def _():
            wait_bytes(idb.at[4], t_ix.at[0])

        @pl.when(x % 2 == 1)
        def _():
            wait_bytes(buf.at[4, pl.ds(0, PR)], t_x.at[0])

        for d in range(4):
            @pl.when(out_any[d])
            def _():
                wait_bytes(idb.at[0], t_itree.at[d])
                wait_bytes(buf.at[0], t_tree.at[d])

        for g in range(4):
            if g % 2 == 0:
                @pl.when(jnp.logical_not(sources[g]))
                def _():
                    wait_bytes(idb.at[g], t_ito0.at[g])
                    wait_bytes(buf.at[g], t_to0.at[g])
        wait_bytes(idb.at[4], t_ito0.at[4])
        wait_bytes(buf.at[4], t_to0.at[4])
        wait_bytes(ch, s_ch)


def chunk_of_block(blk, k):
    return blk.at[k // PARTS, pl.ds((k % PARTS) * PART, PART)]


def split(a):
    high = a.astype(jnp.bfloat16)
    rest = a - high.astype(F32)
    middle = rest.astype(jnp.bfloat16)
    return high, middle, (rest - middle.astype(F32)).astype(jnp.bfloat16)


def left_terms(h, m, low):
    return [h, h, m, h, m, low]


def right_terms(h, m, low):
    return [h, m, h, low, m, h]


def stacked_dot(left, right):
    return lax.dot_general(
        jnp.concatenate(left, axis=1), jnp.concatenate(right, axis=1),
        (((1,), (1,)), ((), ())), preferred_element_type=F32,
    )


def local_kernel(
    bmap, idb, blk, buf, ch, out,
    vb, pan, chv, parts, inv_parts, prod, where_to, slot_for, s_in, s_out, s_pan, s_ch,
):
    w = lax.axis_index("wide")
    n = lax.axis_index("narrow")
    core = w % 2
    slots = blk.shape[0]
    slot_of = [jnp.int32(4)] + [jnp.where(n == w + 8 * h, 4, 2 * h + core) for h in range(2)]
    copies = [pltpu.make_async_copy(ch, chv, s_ch)]
    for column in range(2):
        for q in range(3):
            copies.append(
                pltpu.make_async_copy(
                    buf.at[slot_of[q], pl.ds(column * PR, PR)], pan.at[column, pl.ds(q * PR, PR)], s_pan.at[column, q]
                )
            )
    for copy in copies:
        copy.start()

    def find(slot, column, block_row):
        found = jnp.int32(-1)
        for i in range(PR):
            found = jnp.where(idb[slot, column, 0, i] == block_row, i, found)
        return found

    @pl.loop(0, 2 * PR * PR)
    def _(pair):
        slot_for[pair] = -1

    @pl.loop(0, slots)
    def _(s):
        r, c = bmap[0, s], bmap[1, s]
        h = (c % 16) // 8
        i, j = find(4, 1, r), find(jnp.where(h == 0, slot_of[1], slot_of[2]), 1, c)
        updated = (c > 1) & (i >= 0) & (j >= 0)
        code = jnp.where(updated, i + PR * (j + PR * h), -1)
        code = jnp.where(c == 0, 32 + find(4, 0, r), jnp.where(c == 1, 32 + i, code))
        where_to[s] = code

        @pl.when(updated)
        def _():
            slot_for[jnp.maximum(code, 0)] = s

        @pl.when(code < 32)
        def _():
            pltpu.make_async_copy(blk.at[s], vb.at[s], s_in.at[s]).start()

    for copy in copies[:4]:
        copy.wait()

    first_inv = split(chv[1])
    for k in range(3):
        inv_parts[:, k * W : (k + 1) * W] = first_inv[k]
    second_inv = split(chv[4])
    coupling = split(-dot_nn(chv[4], chv[2]))
    for k in range(3):
        inv_parts[:, (3 + k) * W : (4 + k) * W] = second_inv[k]
        inv_parts[:, (6 + k) * W : (7 + k) * W] = coupling[k]

    def inverse(t):
        return [inv_parts[:, (3 * t + k) * W : (3 * t + k + 1) * W] for k in range(3)]

    @pl.loop(0, 3 * PR // 2)
    def _(b):
        old = pan[0, pl.ds(2 * b, 2)].reshape(2 * W, W)
        value = stacked_dot(left_terms(*split(old)), right_terms(*inverse(0)))
        pan[0, pl.ds(2 * b, 2)] = value.reshape(2, W, W)

    for copy in copies[4:]:
        copy.wait()

    @pl.loop(0, slots)
    def _(s):
        @pl.when(where_to[s] < 0)
        def _():
            pltpu.make_async_copy(blk.at[s], vb.at[s], s_in.at[s]).wait()
            pltpu.make_async_copy(vb.at[s], out.at[s], s_out).start()

    @pl.loop(0, 3 * PR // 2)
    def _(b):
        q = b // 2
        slot = jnp.where(q == 0, slot_of[0], jnp.where(q == 1, slot_of[1], slot_of[2]))
        firsts = []
        for d in range(2):
            block_row = idb[slot, 1, 0, (2 * b + d) % PR]
            i = find(slot, 0, block_row)
            value = pan[0, q * PR + jnp.maximum(i, 0)]
            firsts.append(jnp.where((i >= 0) & (block_row > 0), value, 0.0))
        first = split(jnp.concatenate(firsts, axis=0))
        old = split(pan[1, pl.ds(2 * b, 2)].reshape(2 * W, W))
        value = stacked_dot(
            left_terms(*old) + left_terms(*first), right_terms(*inverse(1)) + right_terms(*inverse(2))
        )
        pan[1, pl.ds(2 * b, 2)] = value.reshape(2, W, W)
        second = split(value)
        for k, part in enumerate((first[0], first[1], second[0], second[1])):
            parts[pl.ds(2 * b, 2), :, k * W : (k + 1) * W] = part.reshape(2, W, W)

    def part(at, count, k):
        return parts[at, :, k * W : (k + 1) * W].reshape(count * W, W)

    def leave(s):
        pltpu.make_async_copy(vb.at[s], out.at[s], s_out).start()

    @pl.loop(0, PR)
    def _(s):
        code = where_to[s]

        @pl.when(code >= 32)
        def _():
            r, c = bmap[0, s], bmap[1, s]

            @pl.when(r == c)
            def _():
                vb[s] = chv[3 * c]

            @pl.when(r != c)
            def _():
                vb[s] = pan[c, code - 32]

            leave(s)

    @pl.loop(0, 2 * PR * PR // 2)
    def _(t):
        j, half = t // (PR // 2), t % (PR // 2)
        held = [slot_for[PR * j + 2 * half + d] for d in range(2)]

        @pl.when((held[0] >= 0) | (held[1] >= 0))
        def _():
            left = [part(pl.ds(2 * half, 2), 2, k) for k in (0, 0, 1, 2, 2, 3)]
            right = [part(pl.ds(PR + j, 1), 1, k) for k in (0, 1, 0, 2, 3, 2)]
            prod[...] = stacked_dot(left, right).reshape(2, W, W)
            for d in range(2):
                @pl.when(held[d] >= 0)
                def _():
                    s = jnp.maximum(held[d], 0)
                    pltpu.make_async_copy(blk.at[s], vb.at[s], s_in.at[s]).wait()
                    vb[s] = vb[s] - prod[d]
                    leave(s)

    pltpu.make_async_copy(out, out, s_out).wait()


def on_device(blocks, block_map):
    ids = block_map.T
    anywhere = pl.BlockSpec(memory_space=pltpu.HBM)
    dma = pltpu.SemaphoreType.DMA
    vmem = pltpu.VMEM
    buf, idb, ch = pl.pallas_call(
        send_kernel,
        out_shape=[
            jax.ShapeDtypeStruct((5, 2 * PR, W, W), F32),
            jax.ShapeDtypeStruct((5, 2) + ids.shape, jnp.int32),
            jax.ShapeDtypeStruct((5, W, W), F32),
        ],
        in_specs=[anywhere, anywhere],
        out_specs=[anywhere, anywhere, anywhere],
        scratch_shapes=[
            vmem((W, W), F32), vmem((3, ROWS, W), F32), vmem((PR, W, W), F32), vmem((3, W, W), F32), vmem((5, W, W), F32),
            vmem((H, H), F32), vmem((H, H), F32), vmem((H, H), F32), vmem((H, H), F32),
            dma((CHUNKS,)), dma((4, CHUNKS)), dma, dma((4,)), dma, dma((3,)), dma((3,)), dma((6,)), dma,
            dma((2,)), dma((4,)), dma((2,)), dma((4,)), dma((5,)), dma((5,)), dma, dma((3,)), dma((3,)), dma((3,)),
            dma((2,)), dma((2,)),
        ],
        compiler_params=pltpu.CompilerParams(collective_id=0, has_side_effects=True, vmem_limit_bytes=60 * 2**20),
    )(blocks, ids)
    slots = blocks.shape[0]
    return pl.pallas_call(
        local_kernel,
        out_shape=jax.ShapeDtypeStruct(blocks.shape, F32),
        in_specs=[
            pl.BlockSpec(memory_space=pltpu.SMEM), pl.BlockSpec(memory_space=pltpu.SMEM), anywhere, anywhere, anywhere,
        ],
        out_specs=anywhere,
        scratch_shapes=[
            vmem((slots, W, W), F32), vmem((2, 3 * PR, W, W), F32), vmem((5, W, W), F32),
            vmem((3 * PR, W, 4 * W), jnp.bfloat16), vmem((W, 9 * W), jnp.bfloat16), vmem((2, W, W), F32),
            pltpu.SMEM((slots,), jnp.int32), pltpu.SMEM((2 * PR * PR,), jnp.int32),
            dma((slots,)), dma, dma((2, 3)), dma,
        ],
        compiler_params=pltpu.CompilerParams(vmem_limit_bytes=60 * 2**20),
    )(ids, idb, blocks, buf, ch)


def solution(mesh):
    return jax.shard_map(
        on_device,
        mesh=mesh,
        in_specs=(P(("wide", "narrow"), None, None), P(("wide", "narrow"), None)),
        out_specs=P(("wide", "narrow"), None, None),
        check_vma=False,
    )
```

```python
import jax
import jax.numpy as jnp
from jax import lax
from jax.experimental import pallas as pl
from jax.experimental.pallas import tpu as pltpu
from jax.sharding import PartitionSpec as P

PR = 4
W = 256
H = 128
G = 8
CHUNKS = 32
PARTS = CHUNKS // (2 * PR)
PART = W // PARTS
RING = 4
ROWS = 16
CHILDREN = (85, 40969, 4097, 32857)
DEPTH = (23130, 60356, 1056)
SKEW = 5
MESH = pl.DeviceIdType.MESH
HIGHEST = lax.Precision.HIGHEST
F32 = jnp.float32


def dot_nn(a, b):
    return lax.dot_general(a, b, (((1,), (0,)), ((), ())), precision=HIGHEST, preferred_element_type=F32)


def dot_nt(a, b):
    return lax.dot_general(a, b, (((1,), (1,)), ((), ())), precision=HIGHEST, preferred_element_type=F32)


def tree_sum(terms):
    terms = list(terms)
    while len(terms) > 1:
        terms = [terms[i] + terms[i + 1] if i + 1 < len(terms) else terms[i] for i in range(0, len(terms), 2)]
    return terms[0]


def eliminate(p, c_ref, u_ref, x_ref):
    lo = p * G
    lane = lax.broadcasted_iota(jnp.int32, (G, H), 1)
    sub = lax.broadcasted_iota(jnp.int32, (G, H), 0)
    rows = c_ref[lo : lo + G, :]
    cols = [jnp.broadcast_to(rows[:, lo + j : lo + j + 1], (G, H)) for j in range(G)]
    a = {(i, j): jnp.broadcast_to(cols[j][i : i + 1, :], (G, H)) for j in range(G) for i in range(j, G)}
    low, inv, x = {}, [None] * G, {}
    for j in range(G):
        inv[j] = lax.rsqrt(a[j, j])
        for i in range(j + 1, G):
            low[i, j] = a[i, j] * inv[j]
        for k in range(j + 1, G):
            for i in range(k, G):
                a[i, k] = a[i, k] - low[i, j] * low[k, j]
    for j in range(G):
        x[j, j] = inv[j]
        for i in range(j + 1, G):
            x[i, j] = -(inv[i] * tree_sum([low[i, k] * x[k, j] for k in range(j, i)]))
    in_block = (lane >= lo) & (lane < lo + G)
    rows_with_eye = jnp.where(in_block, (lane - lo == sub).astype(F32), rows)

    def column(entry, ids):
        out = jnp.zeros((G, H), F32)
        for i in ids:
            out = jnp.where(sub == i, entry(i), out)
        return out

    def row(v, k):
        return jnp.broadcast_to(v[k : k + 1, :], (G, H))

    weights = [column(lambda i: x[i, k], range(k, G)) for k in range(G)]
    weights_t = [column(lambda i: x[k, i], range(0, k + 1)) for k in range(G)]
    reduced = tree_sum([weights[k] * row(rows_with_eye, k) for k in range(G)])
    upper = tree_sum([weights[k] * row(rows, k) for k in range(G)])
    u_ref[lo : lo + G, :] = jnp.where(lane >= lo + sub, upper, 0.0)
    x_ref[lo : lo + G, :] = jnp.where(lane < lo + G, reduced, 0.0)
    solved = tree_sum([weights_t[k] * row(reduced, k) for k in range(G)])
    solved_rows = [row(solved, k) for k in range(G)]
    for m in range(p + 1, H // G):
        old = c_ref[m * G : (m + 1) * G, :]
        taken = [jnp.broadcast_to(old[:, lo + k : lo + k + 1], (G, H)) * solved_rows[k] for k in range(G)]
        c_ref[m * G : (m + 1) * G, :] = jnp.where(in_block, 0.0, old) - tree_sum(taken)


def factor_128(c_ref, u_ref, x_ref):
    for p in range(H // G):
        eliminate(p, c_ref, u_ref, x_ref)


def factor_256(src, low_ref, inv_ref, c_ref, u_ref, x_ref, g_ref):
    zero = jnp.zeros((H, H), F32)
    c_ref[...] = src[0:H, 0:H]
    factor_128(c_ref, u_ref, x_ref)
    x1 = x_ref[...]
    inv_ref[0:H, 0:H] = x1
    inv_ref[0:H, H:W] = zero
    low_ref[0:H, 0:H] = u_ref[...].T
    low_ref[0:H, H:W] = zero
    below = dot_nt(src[H:W, 0:H], x1)
    low_ref[H:W, 0:H] = below
    c_ref[...] = src[H:W, H:W] - dot_nt(below, below)
    g_ref[...] = dot_nn(below, x1)
    factor_128(c_ref, u_ref, x_ref)
    x2 = x_ref[...]
    inv_ref[H:W, H:W] = x2
    low_ref[H:W, H:W] = u_ref[...].T
    inv_ref[H:W, 0:H] = -dot_nn(x2, g_ref[...])


def send_kernel(
    blk, idt, buf, idb, ch,
    dsrc, dpiece, held, dfull, chv, c_ref, u_ref, x_ref, g_ref,
    rs, ps, ri, pi, s_src, s_piece, s_full, s_to0, s_ch,
    t_x, t_tree, t_ix, t_itree, t_to0, t_ito0, t_src, t_scat, t_dx, t_gath, t_first, t_ch,
):
    w = lax.axis_index("wide")
    n = lax.axis_index("narrow")
    x, core = w // 2, w % 2
    y, z = n // RING, n % RING
    partner = (x * 2 + 1 - core, n)
    barrier = pltpu.get_barrier_semaphore()

    def chunk(ref, slot, k):
        return ref.at[slot, k // PARTS, pl.ds(pl.multiple_of((k % PARTS) * PART, PART), PART)]

    def remote(src, dst, send, recv, device):
        return pltpu.make_async_remote_copy(
            src_ref=src, dst_ref=dst, send_sem=send, recv_sem=recv, device_id=device, device_id_type=MESH
        )

    def wait_bytes(ref, sem):
        pltpu.make_async_copy(ref, ref, sem).wait()

    def signal(device):
        pl.semaphore_signal(barrier, inc=1, device_id=device, device_id_type=MESH)

    def at_x(dx):
        return (lax.rem(x + dx, RING) * 2 + 1, n)

    @pl.when(core == 0)
    def _():
        signal(partner)
        for dx in range(1, RING):
            signal((lax.rem(x + dx, RING) * 2, n))

        @pl.loop(0, RING * RING)
        def _(i):
            @pl.when(i != n)
            def _():
                signal((w, i))

        pl.semaphore_wait(barrier, RING * RING + RING - 1)

        def scatter(b, src):
            @pl.loop(0, RING * RING)
            def _(i):
                part = src.at[pl.ds(pl.multiple_of(i * ROWS, ROWS), ROWS)]

                @pl.when(i != n)
                def _():
                    remote(part, dpiece.at[b], t_scat.at[b], s_piece.at[b], (w, i)).start()

                @pl.when(i == n)
                def _():
                    pltpu.make_async_copy(part, dpiece.at[b], s_piece.at[b]).start()

        @pl.when(x == 0)
        def _():
            @pl.when(n == 0)
            def _():
                scatter(0, blk.at[0])

            @pl.when(n == 1)
            def _():
                scatter(1, blk.at[0])

            remote(idt, idb.at[4, 0], t_first.at[0], ri, partner).start()
            for k in range(CHUNKS // 2):
                remote(chunk_of_block(blk, k), chunk(buf, 4, k), t_first.at[1], rs.at[k], partner).start()

            @pl.when(n == 1)
            def _():
                wait_bytes(dsrc, s_src)
                scatter(2, dsrc)

        mine = pl.ds(pl.multiple_of(n * ROWS, ROWS), ROWS)
        for b in range(3):
            wait_bytes(dpiece.at[b], s_piece.at[b])

            @pl.when(x == 0)
            def _():
                for dx in range(1, RING):
                    remote(dpiece.at[b], dpiece.at[b], t_dx.at[b], s_piece.at[b], (dx * 2, n)).start()

            @pl.loop(0, RING * RING)
            def _(i):
                @pl.when(i != n)
                def _():
                    remote(dpiece.at[b], dfull.at[b, mine], t_gath.at[b], s_full.at[b], (w, i)).start()

                @pl.when(i == n)
                def _():
                    pltpu.make_async_copy(dpiece.at[b], dfull.at[b, mine], s_full.at[b]).start()

        wait_bytes(dfull.at[0], s_full.at[0])
        factor_256(dfull.at[0], chv.at[0], chv.at[1], c_ref, u_ref, x_ref, g_ref)
        wait_bytes(dfull.at[1], s_full.at[1])
        l10 = dot_nt(dfull[1], chv[1])
        chv[2] = l10
        wait_bytes(dfull.at[2], s_full.at[2])
        dfull[2] = dfull[2] - dot_nt(l10, l10)
        factor_256(dfull.at[2], chv.at[3], chv.at[4], c_ref, u_ref, x_ref, g_ref)
        chv[5] = -dot_nn(chv[4], chv[2])
        remote(chv, ch, t_ch.at[0], s_ch, partner).start()
        own = pltpu.make_async_copy(chv, ch, t_ch.at[1])
        own.start()

        @pl.when(x == 0)
        def _():
            for b in range(3):
                for dx in range(1, RING):
                    wait_bytes(dpiece.at[b], t_dx.at[b])

            @pl.when(n == 0)
            def _():
                wait_bytes(dfull.at[0, pl.ds(0, W - ROWS)], t_scat.at[0])

            @pl.when(n == 1)
            def _():
                for b in (1, 2):
                    wait_bytes(dfull.at[b, pl.ds(0, W - ROWS)], t_scat.at[b])

            wait_bytes(idt, t_first.at[0])
            wait_bytes(buf.at[4, pl.ds(0, PR)], t_first.at[1])

        for b in range(3):
            wait_bytes(dfull.at[b, pl.ds(0, W - ROWS)], t_gath.at[b])
        for h in range(2):
            @pl.when(n != 2 * x + 8 * h)
            def _():
                wait_bytes(idb.at[2 * h], s_to0.at[2 * h])
                wait_bytes(buf.at[2 * h], s_to0.at[2 * h + 1])

        wait_bytes(idb.at[4], s_to0.at[4])
        wait_bytes(buf.at[4], s_to0.at[5])
        wait_bytes(chv, t_ch.at[0])
        own.wait()

    @pl.when(core == 1)
    def _():
        steps = ((1, 0), (RING - 1, 0), (0, 1), (0, RING - 1))
        near = [(w, lax.rem(y + dy, RING) * RING + lax.rem(z + dz, RING)) for dy, dz in steps]
        signal(partner)
        for dx in range(1, RING):
            signal(at_x(dx))
        for device in near:
            signal(device)
        pl.semaphore_wait(barrier, 1 + RING - 1 + len(near))

        @pl.when(x == 0)
        def _():
            @pl.when(n == 1)
            def _():
                remote(blk.at[0], dsrc, t_src, s_src, partner).start()

            pltpu.make_async_copy(idt, idb.at[4, 1], ri).start()
            pltpu.make_async_copy(blk.at[pl.ds(0, PR)], held, t_first.at[0]).start()
            wait_bytes(held, t_first.at[0])
            for k in range(CHUNKS // 2, CHUNKS):
                pltpu.make_async_copy(chunk_of_block(held, k - CHUNKS // 2), chunk(buf, 4, k), rs.at[k]).start()

        y_rel = lax.rem(y - x // 2 + RING, RING)
        z_rel = lax.rem(z - 2 * (x % 2) + RING, RING)
        sources, sends, depths = [], [], []
        for g in range(4):
            h, q = g // 2, g % 2
            y_own = lax.rem(y_rel + 2 * h, RING)
            z_own = z_rel if q == 0 else lax.rem(1 - z_rel + RING, RING)
            index = y_own * RING + z_own
            flags = [(jnp.int32(mask) >> index) & 1 for mask in CHILDREN]
            if q == 1:
                flags[2], flags[3] = flags[3], flags[2]
            depths.append(sum(((jnp.int32(mask) >> index) & 1) << b for b, mask in enumerate(DEPTH)))
            sources.append(index == 0)
            sends.append(flags)

        out_any, out_g, out_slot, out_lag = [], [], [], []
        for d in range(4):
            here = [jnp.where(sources[g], 1, sends[g][d]) for g in range(4)]
            out_any.append(sum(here) > 0)
            out_g.append(sum(g * here[g] for g in range(4)))
            out_slot.append(sum(jnp.where(sources[g], 4, g) * here[g] for g in range(4)))
            out_lag.append(sum(SKEW * depths[g] * here[g] for g in range(4)))
        lags = [jnp.where(sources[g], CHUNKS + 4 * SKEW, SKEW * depths[g]) for g in range(4)]

        def pass_row(part, recv, x_send, x_odd):
            wait_bytes(part, recv)

            @pl.when(x == 0)
            def _():
                for j, dx in enumerate((1, RING - 1)):
                    remote(part, part, x_send.at[j], recv, at_x(dx)).start()

            @pl.when(x == 1 + 2 * x_odd)
            def _():
                remote(part, part, x_send.at[0], recv, (5, n)).start()

        def block_over(slot, k, send, recv):
            @pl.when(k % PARTS == PARTS - 1)
            def _():
                block = buf.at[slot, k // PARTS]
                remote(block, block, send, recv, partner).start()

        @pl.loop(0, CHUNKS + 4 * SKEW)
        def _(t):
            @pl.when(t < CHUNKS)
            def _():
                k = jnp.minimum(t, CHUNKS - 1)

                @pl.when(t == 0)
                def _():
                    pass_row(idb.at[4], ri, t_ix, 0)
                    remote(idb.at[4], idb.at[4], t_ito0.at[4], s_to0.at[4], partner).start()

                pass_row(chunk(buf, 4, k), rs.at[k], t_x, k % 2)

            for g in range(4):
                late = t - lags[g]

                @pl.when((late >= 0) & (late < CHUNKS))
                def _():
                    k = jnp.minimum(jnp.maximum(late, 0), CHUNKS - 1)
                    wait_bytes(chunk(buf, g, k), ps.at[g, k])

                    @pl.when(late == 0)
                    def _():
                        wait_bytes(idb.at[g], pi.at[g])
                        if g % 2 == 0:
                            remote(idb.at[g], idb.at[g], t_ito0.at[g], s_to0.at[g], partner).start()

            for d in range(4):
                late = t - out_lag[d]

                @pl.when(out_any[d] & (late >= 0) & (late < CHUNKS))
                def _():
                    k = jnp.minimum(jnp.maximum(late, 0), CHUNKS - 1)
                    g, slot = out_g[d], out_slot[d]

                    @pl.when(late == 0)
                    def _():
                        remote(idb.at[slot], idb.at[g], t_itree.at[d], pi.at[g], near[d]).start()

                    remote(chunk(buf, slot, k), chunk(buf, g, k), t_tree.at[d], ps.at[g, k], near[d]).start()

            @pl.when(t < CHUNKS)
            def _():
                block_over(4, jnp.minimum(t, CHUNKS - 1), t_to0.at[4], s_to0.at[5])

            for g in (0, 2):
                late = t - lags[g]

                @pl.when((late >= 0) & (late < CHUNKS))
                def _():
                    block_over(g, jnp.minimum(jnp.maximum(late, 0), CHUNKS - 1), t_to0.at[g], s_to0.at[g + 1])

        @pl.when(x == 0)
        def _():
            for j in range(2):
                wait_bytes(idb.at[4], t_ix.at[j])
                wait_bytes(buf.at[4], t_x.at[j])
            @pl.when(n == 1)
            def _():
                wait_bytes(dsrc, t_src)

        @pl.when(x == 1)
        def _():
            wait_bytes(idb.at[4], t_ix.at[0])

        @pl.when(x % 2 == 1)
        def _():
            wait_bytes(buf.at[4, pl.ds(0, PR)], t_x.at[0])

        for d in range(4):
            @pl.when(out_any[d])
            def _():
                wait_bytes(idb.at[0], t_itree.at[d])
                wait_bytes(buf.at[0], t_tree.at[d])

        for g in range(4):
            if g % 2 == 0:
                @pl.when(jnp.logical_not(sources[g]))
                def _():
                    wait_bytes(idb.at[g], t_ito0.at[g])
                    wait_bytes(buf.at[g], t_to0.at[g])
        wait_bytes(idb.at[4], t_ito0.at[4])
        wait_bytes(buf.at[4], t_to0.at[4])
        wait_bytes(ch, s_ch)


def chunk_of_block(blk, k):
    return blk.at[k // PARTS, pl.ds((k % PARTS) * PART, PART)]


def split(a):
    high = a.astype(jnp.bfloat16)
    rest = a - high.astype(F32)
    middle = rest.astype(jnp.bfloat16)
    return high, middle, (rest - middle.astype(F32)).astype(jnp.bfloat16)


def left_terms(h, m, low):
    return [h, h, m, h, m, low]


def right_terms(h, m, low):
    return [h, m, h, low, m, h]


def stacked_dot(left, right):
    return lax.dot_general(
        jnp.concatenate(left, axis=1), jnp.concatenate(right, axis=1),
        (((1,), (1,)), ((), ())), preferred_element_type=F32,
    )


def local_kernel(
    bmap, idb, blk, buf, ch, out,
    vb, pan, chv, parts, inv_parts, prod, where_to, slot_for, s_in, s_out, s_pan, s_ch,
):
    w = lax.axis_index("wide")
    n = lax.axis_index("narrow")
    core = w % 2
    slots = blk.shape[0]
    slot_of = [jnp.int32(4)] + [jnp.where(n == w + 8 * h, 4, 2 * h + core) for h in range(2)]
    copies = [pltpu.make_async_copy(ch, chv, s_ch)]
    for column in range(2):
        for q in range(3):
            copies.append(
                pltpu.make_async_copy(
                    buf.at[slot_of[q], pl.ds(column * PR, PR)], pan.at[column, pl.ds(q * PR, PR)], s_pan.at[column, q]
                )
            )
    for copy in copies:
        copy.start()

    ids = [[[idb[slot_of[q], column, 0, i] for i in range(PR)] for q in range(3)] for column in range(2)]

    def find(rows, block_row):
        found = jnp.int32(-1)
        for i, held_row in enumerate(rows):
            found = jnp.where(held_row == block_row, i, found)
        return found

    @pl.loop(0, 2 * PR * PR)
    def _(pair):
        slot_for[pair] = -1

    @pl.loop(0, slots)
    def _(s):
        r, c = bmap[0, s], bmap[1, s]
        i, j = find(ids[1][0], r), find(ids[1][1] + ids[1][2], c)
        updated = (c > 1) & (i >= 0) & (j >= 0)
        code = jnp.where(updated, i + PR * j, -1)
        code = jnp.where(c == 0, 32 + find(ids[0][0], r), jnp.where(c == 1, 32 + i, code))
        where_to[s] = code

        @pl.when(updated)
        def _():
            slot_for[jnp.maximum(code, 0)] = s

        @pl.when(code < 32)
        def _():
            pltpu.make_async_copy(blk.at[s], vb.at[s], s_in.at[s]).start()

    for copy in copies[:4]:
        copy.wait()

    first_inv = split(chv[1])
    for k in range(3):
        inv_parts[:, k * W : (k + 1) * W] = first_inv[k]
    second_inv = split(chv[4])
    coupling = split(chv[5])
    for k in range(3):
        inv_parts[:, (3 + k) * W : (4 + k) * W] = second_inv[k]
        inv_parts[:, (6 + k) * W : (7 + k) * W] = coupling[k]

    def inverse(t):
        return [inv_parts[:, (3 * t + k) * W : (3 * t + k + 1) * W] for k in range(3)]

    for b in range(3 * PR // 2):
        old = pan[0, pl.ds(2 * b, 2)].reshape(2 * W, W)
        value = stacked_dot(left_terms(*split(old)), right_terms(*inverse(0)))
        pan[0, pl.ds(2 * b, 2)] = value.reshape(2, W, W)

    for copy in copies[4:]:
        copy.wait()

    for b in range(3 * PR // 2):
        q = b // 2
        firsts = []
        for d in range(2):
            block_row = ids[1][q][(2 * b + d) % PR]
            i = find(ids[0][q], block_row)
            value = pan[0, q * PR + jnp.maximum(i, 0)]
            firsts.append(jnp.where((i >= 0) & (block_row > 0), value, 0.0))
        first = split(jnp.concatenate(firsts, axis=0))
        old = split(pan[1, pl.ds(2 * b, 2)].reshape(2 * W, W))
        value = stacked_dot(
            left_terms(*old) + left_terms(*first), right_terms(*inverse(1)) + right_terms(*inverse(2))
        )
        pan[1, pl.ds(2 * b, 2)] = value.reshape(2, W, W)
        second = split(value)
        for k, part in enumerate((first[0], first[1], second[0], second[1])):
            parts[pl.ds(2 * b, 2), :, k * W : (k + 1) * W] = part.reshape(2, W, W)

    @pl.loop(0, slots)
    def _(s):
        @pl.when(where_to[s] < 0)
        def _():
            pltpu.make_async_copy(blk.at[s], vb.at[s], s_in.at[s]).wait()
            pltpu.make_async_copy(vb.at[s], out.at[s], s_out).start()

    def part(at, count, k):
        return parts[at, :, k * W : (k + 1) * W].reshape(count * W, W)

    def leave(s):
        pltpu.make_async_copy(vb.at[s], out.at[s], s_out).start()

    @pl.loop(0, PR)
    def _(s):
        code = where_to[s]

        @pl.when(code >= 32)
        def _():
            r, c = bmap[0, s], bmap[1, s]

            @pl.when(r == c)
            def _():
                vb[s] = chv[3 * c]

            @pl.when(r != c)
            def _():
                vb[s] = pan[c, code - 32]

            leave(s)

    @pl.loop(0, 2 * PR * PR // 2)
    def _(t):
        j, half = t // (PR // 2), t % (PR // 2)
        held = [slot_for[PR * j + 2 * half + d] for d in range(2)]

        @pl.when((held[0] >= 0) | (held[1] >= 0))
        def _():
            left = [part(pl.ds(2 * half, 2), 2, k) for k in (0, 0, 1, 2, 2, 3)]
            right = [part(pl.ds(PR + j, 1), 1, k) for k in (0, 1, 0, 2, 3, 2)]
            prod[...] = stacked_dot(left, right).reshape(2, W, W)
            for d in range(2):
                @pl.when(held[d] >= 0)
                def _():
                    s = jnp.maximum(held[d], 0)
                    pltpu.make_async_copy(blk.at[s], vb.at[s], s_in.at[s]).wait()
                    vb[s] = vb[s] - prod[d]
                    leave(s)

    pltpu.make_async_copy(out, out, s_out).wait()


def on_device(blocks, block_map):
    ids = block_map.T
    anywhere = pl.BlockSpec(memory_space=pltpu.HBM)
    dma = pltpu.SemaphoreType.DMA
    vmem = pltpu.VMEM
    buf, idb, ch = pl.pallas_call(
        send_kernel,
        out_shape=[
            jax.ShapeDtypeStruct((5, 2 * PR, W, W), F32),
            jax.ShapeDtypeStruct((5, 2) + ids.shape, jnp.int32),
            jax.ShapeDtypeStruct((6, W, W), F32),
        ],
        in_specs=[anywhere, anywhere],
        out_specs=[anywhere, anywhere, anywhere],
        scratch_shapes=[
            vmem((W, W), F32), vmem((3, ROWS, W), F32), vmem((PR, W, W), F32), vmem((3, W, W), F32), vmem((6, W, W), F32),
            vmem((H, H), F32), vmem((H, H), F32), vmem((H, H), F32), vmem((H, H), F32),
            dma((CHUNKS,)), dma((4, CHUNKS)), dma, dma((4,)), dma, dma((3,)), dma((3,)), dma((6,)), dma,
            dma((2,)), dma((4,)), dma((2,)), dma((4,)), dma((5,)), dma((5,)), dma, dma((3,)), dma((3,)), dma((3,)),
            dma((2,)), dma((2,)),
        ],
        compiler_params=pltpu.CompilerParams(collective_id=0, has_side_effects=True, vmem_limit_bytes=60 * 2**20),
    )(blocks, ids)
    slots = blocks.shape[0]
    return pl.pallas_call(
        local_kernel,
        out_shape=jax.ShapeDtypeStruct(blocks.shape, F32),
        in_specs=[
            pl.BlockSpec(memory_space=pltpu.SMEM), pl.BlockSpec(memory_space=pltpu.SMEM), anywhere, anywhere, anywhere,
        ],
        out_specs=anywhere,
        scratch_shapes=[
            vmem((slots, W, W), F32), vmem((2, 3 * PR, W, W), F32), vmem((6, W, W), F32),
            vmem((3 * PR, W, 4 * W), jnp.bfloat16), vmem((W, 9 * W), jnp.bfloat16), vmem((2, W, W), F32),
            pltpu.SMEM((slots,), jnp.int32), pltpu.SMEM((2 * PR * PR,), jnp.int32),
            dma((slots,)), dma, dma((2, 3)), dma,
        ],
        compiler_params=pltpu.CompilerParams(vmem_limit_bytes=60 * 2**20),
    )(ids, idb, blocks, buf, ch)


def solution(mesh):
    return jax.shard_map(
        on_device,
        mesh=mesh,
        in_specs=(P(("wide", "narrow"), None, None), P(("wide", "narrow"), None)),
        out_specs=P(("wide", "narrow"), None, None),
        check_vma=False,
    )
```

```python
import jax
import jax.numpy as jnp
from jax import lax
from jax.experimental import pallas as pl
from jax.experimental.pallas import tpu as pltpu
from jax.sharding import PartitionSpec as P

PR = 4
W = 256
H = 128
G = 8
CHUNKS = 32
PARTS = CHUNKS // (2 * PR)
PART = W // PARTS
RING = 4
ROWS = 16
CHILDREN = (85, 40969, 4097, 32857)
DEPTH = (23130, 60356, 1056)
SKEW = 5
MESH = pl.DeviceIdType.MESH
HIGHEST = lax.Precision.HIGHEST
F32 = jnp.float32


def dot_nn(a, b):
    return lax.dot_general(a, b, (((1,), (0,)), ((), ())), precision=HIGHEST, preferred_element_type=F32)


def dot_nt(a, b):
    return lax.dot_general(a, b, (((1,), (1,)), ((), ())), precision=HIGHEST, preferred_element_type=F32)


def tree_sum(terms):
    terms = list(terms)
    while len(terms) > 1:
        terms = [terms[i] + terms[i + 1] if i + 1 < len(terms) else terms[i] for i in range(0, len(terms), 2)]
    return terms[0]


def eliminate(p, c_ref, u_ref, x_ref):
    lo = p * G
    lane = lax.broadcasted_iota(jnp.int32, (G, H), 1)
    sub = lax.broadcasted_iota(jnp.int32, (G, H), 0)
    rows = c_ref[lo : lo + G, :]
    cols = [jnp.broadcast_to(rows[:, lo + j : lo + j + 1], (G, H)) for j in range(G)]
    a = {(i, j): jnp.broadcast_to(cols[j][i : i + 1, :], (G, H)) for j in range(G) for i in range(j, G)}
    low, inv, x = {}, [None] * G, {}
    for j in range(G):
        inv[j] = lax.rsqrt(a[j, j])
        for i in range(j + 1, G):
            low[i, j] = a[i, j] * inv[j]
        for k in range(j + 1, G):
            for i in range(k, G):
                a[i, k] = a[i, k] - low[i, j] * low[k, j]
    for j in range(G):
        x[j, j] = inv[j]
        for i in range(j + 1, G):
            x[i, j] = -(inv[i] * tree_sum([low[i, k] * x[k, j] for k in range(j, i)]))
    in_block = (lane >= lo) & (lane < lo + G)
    rows_with_eye = jnp.where(in_block, (lane - lo == sub).astype(F32), rows)

    def column(entry, ids):
        out = jnp.zeros((G, H), F32)
        for i in ids:
            out = jnp.where(sub == i, entry(i), out)
        return out

    def row(v, k):
        return jnp.broadcast_to(v[k : k + 1, :], (G, H))

    weights = [column(lambda i: x[i, k], range(k, G)) for k in range(G)]
    weights_t = [column(lambda i: x[k, i], range(0, k + 1)) for k in range(G)]
    reduced = tree_sum([weights[k] * row(rows_with_eye, k) for k in range(G)])
    upper = tree_sum([weights[k] * row(rows, k) for k in range(G)])
    u_ref[lo : lo + G, :] = jnp.where(lane >= lo + sub, upper, 0.0)
    x_ref[lo : lo + G, :] = jnp.where(lane < lo + G, reduced, 0.0)
    solved = tree_sum([weights_t[k] * row(reduced, k) for k in range(G)])
    solved_rows = [row(solved, k) for k in range(G)]
    for m in range(p + 1, H // G):
        old = c_ref[m * G : (m + 1) * G, :]
        taken = [jnp.broadcast_to(old[:, lo + k : lo + k + 1], (G, H)) * solved_rows[k] for k in range(G)]
        c_ref[m * G : (m + 1) * G, :] = jnp.where(in_block, 0.0, old) - tree_sum(taken)


def factor_128(c_ref, u_ref, x_ref):
    for p in range(H // G):
        eliminate(p, c_ref, u_ref, x_ref)


def factor_256(src, low_ref, inv_ref, c_ref, u_ref, x_ref, g_ref):
    zero = jnp.zeros((H, H), F32)
    c_ref[...] = src[0:H, 0:H]
    factor_128(c_ref, u_ref, x_ref)
    x1 = x_ref[...]
    inv_ref[0:H, 0:H] = x1
    inv_ref[0:H, H:W] = zero
    low_ref[0:H, 0:H] = u_ref[...].T
    low_ref[0:H, H:W] = zero
    below = dot_nt(src[H:W, 0:H], x1)
    low_ref[H:W, 0:H] = below
    c_ref[...] = src[H:W, H:W] - dot_nt(below, below)
    g_ref[...] = dot_nn(below, x1)
    factor_128(c_ref, u_ref, x_ref)
    x2 = x_ref[...]
    inv_ref[H:W, H:W] = x2
    low_ref[H:W, H:W] = u_ref[...].T
    inv_ref[H:W, 0:H] = -dot_nn(x2, g_ref[...])


def send_kernel(
    blk, idt, buf, idb, ch,
    dsrc, dpiece, held, dfull, chv, c_ref, u_ref, x_ref, g_ref,
    rs, ps, ri, pi, s_src, s_piece, s_full, s_to0, s_ch,
    t_x, t_tree, t_ix, t_itree, t_to0, t_ito0, t_src, t_scat, t_dx, t_gath, t_first, t_ch,
):
    w = lax.axis_index("wide")
    n = lax.axis_index("narrow")
    x, core = w // 2, w % 2
    y, z = n // RING, n % RING
    partner = (x * 2 + 1 - core, n)
    barrier = pltpu.get_barrier_semaphore()

    def chunk(ref, slot, k):
        return ref.at[slot, k // PARTS, pl.ds(pl.multiple_of((k % PARTS) * PART, PART), PART)]

    def remote(src, dst, send, recv, device):
        return pltpu.make_async_remote_copy(
            src_ref=src, dst_ref=dst, send_sem=send, recv_sem=recv, device_id=device, device_id_type=MESH
        )

    def wait_bytes(ref, sem):
        pltpu.make_async_copy(ref, ref, sem).wait()

    def signal(device):
        pl.semaphore_signal(barrier, inc=1, device_id=device, device_id_type=MESH)

    def at_x(dx):
        return (lax.rem(x + dx, RING) * 2 + 1, n)

    @pl.when(core == 0)
    def _():
        signal(partner)
        for dx in range(1, RING):
            signal((lax.rem(x + dx, RING) * 2, n))

        @pl.loop(0, RING * RING)
        def _(i):
            @pl.when(i != n)
            def _():
                signal((w, i))

        pl.semaphore_wait(barrier, RING * RING + RING - 1)

        def scatter(b, src):
            @pl.loop(0, RING * RING)
            def _(i):
                part = src.at[pl.ds(pl.multiple_of(i * ROWS, ROWS), ROWS)]

                @pl.when(i != n)
                def _():
                    remote(part, dpiece.at[b], t_scat.at[b], s_piece.at[b], (w, i)).start()

                @pl.when(i == n)
                def _():
                    pltpu.make_async_copy(part, dpiece.at[b], s_piece.at[b]).start()

        @pl.when(x == 0)
        def _():
            @pl.when(n == 0)
            def _():
                scatter(0, blk.at[0])

            @pl.when(n == 1)
            def _():
                scatter(1, blk.at[0])

            remote(idt, idb.at[4, 0], t_first.at[0], ri, partner).start()
            for k in range(CHUNKS // 2):
                remote(chunk_of_block(blk, k), chunk(buf, 4, k), t_first.at[1], rs.at[k], partner).start()

            @pl.when(n == 1)
            def _():
                wait_bytes(dsrc, s_src)
                scatter(2, dsrc)

        mine = pl.ds(pl.multiple_of(n * ROWS, ROWS), ROWS)
        for b in range(3):
            wait_bytes(dpiece.at[b], s_piece.at[b])

            @pl.when(x == 0)
            def _():
                for dx in range(1, RING):
                    remote(dpiece.at[b], dpiece.at[b], t_dx.at[b], s_piece.at[b], (dx * 2, n)).start()

            @pl.loop(0, RING * RING)
            def _(i):
                @pl.when(i != n)
                def _():
                    remote(dpiece.at[b], dfull.at[b, mine], t_gath.at[b], s_full.at[b], (w, i)).start()

                @pl.when(i == n)
                def _():
                    pltpu.make_async_copy(dpiece.at[b], dfull.at[b, mine], s_full.at[b]).start()

        wait_bytes(dfull.at[0], s_full.at[0])
        factor_256(dfull.at[0], chv.at[0], chv.at[1], c_ref, u_ref, x_ref, g_ref)
        wait_bytes(dfull.at[1], s_full.at[1])
        l10 = dot_nt(dfull[1], chv[1])
        chv[2] = l10
        wait_bytes(dfull.at[2], s_full.at[2])
        dfull[2] = dfull[2] - dot_nt(l10, l10)
        factor_256(dfull.at[2], chv.at[3], chv.at[4], c_ref, u_ref, x_ref, g_ref)
        chv[5] = -dot_nn(chv[4], chv[2])
        remote(chv, ch, t_ch.at[0], s_ch, partner).start()
        own = pltpu.make_async_copy(chv, ch, t_ch.at[1])
        own.start()

        @pl.when(x == 0)
        def _():
            for b in range(3):
                for dx in range(1, RING):
                    wait_bytes(dpiece.at[b], t_dx.at[b])

            @pl.when(n == 0)
            def _():
                wait_bytes(dfull.at[0, pl.ds(0, W - ROWS)], t_scat.at[0])

            @pl.when(n == 1)
            def _():
                for b in (1, 2):
                    wait_bytes(dfull.at[b, pl.ds(0, W - ROWS)], t_scat.at[b])

            wait_bytes(idt, t_first.at[0])
            wait_bytes(buf.at[4, pl.ds(0, PR)], t_first.at[1])

        for b in range(3):
            wait_bytes(dfull.at[b, pl.ds(0, W - ROWS)], t_gath.at[b])
        for h in range(2):
            @pl.when(n != 2 * x + 8 * h)
            def _():
                wait_bytes(idb.at[2 * h], s_to0.at[2 * h])
                wait_bytes(buf.at[2 * h], s_to0.at[2 * h + 1])

        wait_bytes(idb.at[4], s_to0.at[4])
        wait_bytes(buf.at[4], s_to0.at[5])
        wait_bytes(chv, t_ch.at[0])
        own.wait()

    @pl.when(core == 1)
    def _():
        steps = ((1, 0), (RING - 1, 0), (0, 1), (0, RING - 1))
        near = [(w, lax.rem(y + dy, RING) * RING + lax.rem(z + dz, RING)) for dy, dz in steps]
        signal(partner)
        for dx in range(1, RING):
            signal(at_x(dx))
        for device in near:
            signal(device)
        pl.semaphore_wait(barrier, 1 + RING - 1 + len(near))

        @pl.when(x == 0)
        def _():
            @pl.when(n == 1)
            def _():
                remote(blk.at[0], dsrc, t_src, s_src, partner).start()

            pltpu.make_async_copy(idt, idb.at[4, 1], ri).start()
            pltpu.make_async_copy(blk.at[pl.ds(0, PR)], held, t_first.at[0]).start()
            wait_bytes(held, t_first.at[0])
            for k in range(CHUNKS // 2, CHUNKS):
                pltpu.make_async_copy(chunk_of_block(held, k - CHUNKS // 2), chunk(buf, 4, k), rs.at[k]).start()

        y_rel = lax.rem(y - x // 2 + RING, RING)
        z_rel = lax.rem(z - 2 * (x % 2) + RING, RING)
        sources, sends, depths = [], [], []
        for g in range(4):
            h, q = g // 2, g % 2
            y_own = lax.rem(y_rel + 2 * h, RING)
            z_own = z_rel if q == 0 else lax.rem(1 - z_rel + RING, RING)
            index = y_own * RING + z_own
            flags = [(jnp.int32(mask) >> index) & 1 for mask in CHILDREN]
            if q == 1:
                flags[2], flags[3] = flags[3], flags[2]
            depths.append(sum(((jnp.int32(mask) >> index) & 1) << b for b, mask in enumerate(DEPTH)))
            sources.append(index == 0)
            sends.append(flags)

        out_any, out_g, out_slot, out_lag = [], [], [], []
        for d in range(4):
            here = [jnp.where(sources[g], 1, sends[g][d]) for g in range(4)]
            out_any.append(sum(here) > 0)
            out_g.append(sum(g * here[g] for g in range(4)))
            out_slot.append(sum(jnp.where(sources[g], 4, g) * here[g] for g in range(4)))
            out_lag.append(sum(SKEW * depths[g] * here[g] for g in range(4)))
        lags = [jnp.where(sources[g], CHUNKS + 4 * SKEW, SKEW * depths[g]) for g in range(4)]

        def pass_row(part, recv, x_send, x_odd):
            wait_bytes(part, recv)

            @pl.when(x == 0)
            def _():
                for j, dx in enumerate((1, RING - 1)):
                    remote(part, part, x_send.at[j], recv, at_x(dx)).start()

            @pl.when(x == 1 + 2 * x_odd)
            def _():
                remote(part, part, x_send.at[0], recv, (5, n)).start()

        def block_over(slot, k, send, recv):
            @pl.when(k % PARTS == PARTS - 1)
            def _():
                block = buf.at[slot, k // PARTS]
                remote(block, block, send, recv, partner).start()

        @pl.loop(0, CHUNKS + 4 * SKEW)
        def _(t):
            @pl.when(t < CHUNKS)
            def _():
                k = jnp.minimum(t, CHUNKS - 1)

                @pl.when(t == 0)
                def _():
                    pass_row(idb.at[4], ri, t_ix, 0)
                    remote(idb.at[4], idb.at[4], t_ito0.at[4], s_to0.at[4], partner).start()

                pass_row(chunk(buf, 4, k), rs.at[k], t_x, k % 2)

            for g in range(4):
                late = t - lags[g]

                @pl.when((late >= 0) & (late < CHUNKS))
                def _():
                    k = jnp.minimum(jnp.maximum(late, 0), CHUNKS - 1)
                    wait_bytes(chunk(buf, g, k), ps.at[g, k])

                    @pl.when(late == 0)
                    def _():
                        wait_bytes(idb.at[g], pi.at[g])
                        if g % 2 == 0:
                            remote(idb.at[g], idb.at[g], t_ito0.at[g], s_to0.at[g], partner).start()

            for d in range(4):
                late = t - out_lag[d]

                @pl.when(out_any[d] & (late >= 0) & (late < CHUNKS))
                def _():
                    k = jnp.minimum(jnp.maximum(late, 0), CHUNKS - 1)
                    g, slot = out_g[d], out_slot[d]

                    @pl.when(late == 0)
                    def _():
                        remote(idb.at[slot], idb.at[g], t_itree.at[d], pi.at[g], near[d]).start()

                    remote(chunk(buf, slot, k), chunk(buf, g, k), t_tree.at[d], ps.at[g, k], near[d]).start()

            @pl.when(t < CHUNKS)
            def _():
                block_over(4, jnp.minimum(t, CHUNKS - 1), t_to0.at[4], s_to0.at[5])

            for g in (0, 2):
                late = t - lags[g]

                @pl.when((late >= 0) & (late < CHUNKS))
                def _():
                    block_over(g, jnp.minimum(jnp.maximum(late, 0), CHUNKS - 1), t_to0.at[g], s_to0.at[g + 1])

        @pl.when(x == 0)
        def _():
            for j in range(2):
                wait_bytes(idb.at[4], t_ix.at[j])
                wait_bytes(buf.at[4], t_x.at[j])
            @pl.when(n == 1)
            def _():
                wait_bytes(dsrc, t_src)

        @pl.when(x == 1)
        def _():
            wait_bytes(idb.at[4], t_ix.at[0])

        @pl.when(x % 2 == 1)
        def _():
            wait_bytes(buf.at[4, pl.ds(0, PR)], t_x.at[0])

        for d in range(4):
            @pl.when(out_any[d])
            def _():
                wait_bytes(idb.at[0], t_itree.at[d])
                wait_bytes(buf.at[0], t_tree.at[d])

        for g in range(4):
            if g % 2 == 0:
                @pl.when(jnp.logical_not(sources[g]))
                def _():
                    wait_bytes(idb.at[g], t_ito0.at[g])
                    wait_bytes(buf.at[g], t_to0.at[g])
        wait_bytes(idb.at[4], t_ito0.at[4])
        wait_bytes(buf.at[4], t_to0.at[4])
        wait_bytes(ch, s_ch)


def chunk_of_block(blk, k):
    return blk.at[k // PARTS, pl.ds((k % PARTS) * PART, PART)]


def split(a):
    high = a.astype(jnp.bfloat16)
    rest = a - high.astype(F32)
    middle = rest.astype(jnp.bfloat16)
    return high, middle, (rest - middle.astype(F32)).astype(jnp.bfloat16)


def left_terms(h, m, low):
    return [h, h, m, h, m, low]


def right_terms(h, m, low):
    return [h, m, h, low, m, h]


def stacked_dot(left, right):
    return lax.dot_general(
        jnp.concatenate(left, axis=1), jnp.concatenate(right, axis=1),
        (((1,), (1,)), ((), ())), preferred_element_type=F32,
    )


def local_kernel(
    bmap, idb, blk, buf, ch, out,
    vb, pan, chv, parts, inv_parts, prod, where_to, slot_for, s_in, s_out, s_pan, s_ch,
):
    w = lax.axis_index("wide")
    n = lax.axis_index("narrow")
    core = w % 2
    slots = blk.shape[0]
    slot_of = [jnp.int32(4)] + [jnp.where(n == w + 8 * h, 4, 2 * h + core) for h in range(2)]
    copies = [pltpu.make_async_copy(ch, chv, s_ch)]
    for column in range(2):
        for q in range(3):
            copies.append(
                pltpu.make_async_copy(
                    buf.at[slot_of[q], pl.ds(column * PR, PR)], pan.at[column, pl.ds(q * PR, PR)], s_pan.at[column, q]
                )
            )
    for copy in copies:
        copy.start()

    ids = [[[idb[slot_of[q], column, 0, i] for i in range(PR)] for q in range(3)] for column in range(2)]

    def find(rows, block_row):
        found = jnp.int32(-1)
        for i, held_row in enumerate(rows):
            found = jnp.where(held_row == block_row, i, found)
        return found

    @pl.loop(0, 2 * PR * PR)
    def _(pair):
        slot_for[pair] = -1

    @pl.loop(0, slots)
    def _(s):
        r, c = bmap[0, s], bmap[1, s]
        i, j = find(ids[1][0], r), find(ids[1][1] + ids[1][2], c)
        updated = (c > 1) & (i >= 0) & (j >= 0)
        code = jnp.where(updated, i + PR * j, -1)
        code = jnp.where(c == 0, 32 + find(ids[0][0], r), jnp.where(c == 1, 32 + i, code))
        where_to[s] = code

        @pl.when(updated)
        def _():
            slot_for[jnp.maximum(code, 0)] = s

        @pl.when(code < 32)
        def _():
            pltpu.make_async_copy(blk.at[s], vb.at[s], s_in.at[s]).start()

    for copy in copies[:4]:
        copy.wait()

    first_inv = split(chv[1])
    for k in range(3):
        inv_parts[:, k * W : (k + 1) * W] = first_inv[k]
    second_inv = split(chv[4])
    coupling = split(chv[5])
    for k in range(3):
        inv_parts[:, (3 + k) * W : (4 + k) * W] = second_inv[k]
        inv_parts[:, (6 + k) * W : (7 + k) * W] = coupling[k]

    def inverse(t):
        return [inv_parts[:, (3 * t + k) * W : (3 * t + k + 1) * W] for k in range(3)]

    for b in range(3 * PR // 2):
        old = pan[0, pl.ds(2 * b, 2)].reshape(2 * W, W)
        value = stacked_dot(left_terms(*split(old)), right_terms(*inverse(0)))
        pan[0, pl.ds(2 * b, 2)] = value.reshape(2, W, W)

    for copy in copies[4:]:
        copy.wait()

    for b in range(3 * PR // 2):
        q = b // 2
        firsts = []
        for d in range(2):
            block_row = ids[1][q][(2 * b + d) % PR]
            i = find(ids[0][q], block_row)
            value = pan[0, q * PR + jnp.maximum(i, 0)]
            firsts.append(jnp.where((i >= 0) & (block_row > 0), value, 0.0))
        first = split(jnp.concatenate(firsts, axis=0))
        old = split(pan[1, pl.ds(2 * b, 2)].reshape(2 * W, W))
        value = stacked_dot(
            left_terms(*old) + left_terms(*first), right_terms(*inverse(1)) + right_terms(*inverse(2))
        )
        pan[1, pl.ds(2 * b, 2)] = value.reshape(2, W, W)
        second = split(value)
        for k, part in enumerate((first[0], first[1], second[0], second[1])):
            parts[pl.ds(2 * b, 2), :, k * W : (k + 1) * W] = part.reshape(2, W, W)

    @pl.loop(0, slots)
    def _(s):
        @pl.when(where_to[s] < 0)
        def _():
            pltpu.make_async_copy(blk.at[s], vb.at[s], s_in.at[s]).wait()
            pltpu.make_async_copy(vb.at[s], out.at[s], s_out).start()

    def part(at, count, k):
        return parts[at, :, k * W : (k + 1) * W].reshape(count * W, W)

    def leave(s):
        pltpu.make_async_copy(vb.at[s], out.at[s], s_out).start()

    @pl.loop(0, PR)
    def _(s):
        code = where_to[s]

        @pl.when(code >= 32)
        def _():
            r, c = bmap[0, s], bmap[1, s]

            @pl.when(r == c)
            def _():
                vb[s] = chv[3 * c]

            @pl.when(r != c)
            def _():
                vb[s] = pan[c, code - 32]

            leave(s)

    @pl.loop(0, 2 * PR * PR // 2)
    def _(t):
        j, half = t // (PR // 2), t % (PR // 2)
        held = [slot_for[PR * j + 2 * half + d] for d in range(2)]

        def update(first, count):
            left = [part(pl.ds(2 * half + first, count), count, k) for k in (0, 0, 1, 2, 2, 3)]
            right = [part(pl.ds(PR + j, 1), 1, k) for k in (0, 1, 0, 2, 3, 2)]
            prod[0:count] = stacked_dot(left, right).reshape(count, W, W)
            for d in range(count):
                s = jnp.maximum(held[first] if count == 1 else held[d], 0)
                pltpu.make_async_copy(blk.at[s], vb.at[s], s_in.at[s]).wait()
                vb[s] = vb[s] - prod[d]
                leave(s)

        both = (held[0] >= 0) & (held[1] >= 0)

        @pl.when(both)
        def _():
            update(0, 2)

        for d in range(2):
            @pl.when((held[d] >= 0) & jnp.logical_not(both))
            def _():
                update(d, 1)

    pltpu.make_async_copy(out, out, s_out).wait()


def on_device(blocks, block_map):
    ids = block_map.T
    anywhere = pl.BlockSpec(memory_space=pltpu.HBM)
    dma = pltpu.SemaphoreType.DMA
    vmem = pltpu.VMEM
    buf, idb, ch = pl.pallas_call(
        send_kernel,
        out_shape=[
            jax.ShapeDtypeStruct((5, 2 * PR, W, W), F32),
            jax.ShapeDtypeStruct((5, 2) + ids.shape, jnp.int32),
            jax.ShapeDtypeStruct((6, W, W), F32),
        ],
        in_specs=[anywhere, anywhere],
        out_specs=[anywhere, anywhere, anywhere],
        scratch_shapes=[
            vmem((W, W), F32), vmem((3, ROWS, W), F32), vmem((PR, W, W), F32), vmem((3, W, W), F32), vmem((6, W, W), F32),
            vmem((H, H), F32), vmem((H, H), F32), vmem((H, H), F32), vmem((H, H), F32),
            dma((CHUNKS,)), dma((4, CHUNKS)), dma, dma((4,)), dma, dma((3,)), dma((3,)), dma((6,)), dma,
            dma((2,)), dma((4,)), dma((2,)), dma((4,)), dma((5,)), dma((5,)), dma, dma((3,)), dma((3,)), dma((3,)),
            dma((2,)), dma((2,)),
        ],
        compiler_params=pltpu.CompilerParams(collective_id=0, has_side_effects=True, vmem_limit_bytes=60 * 2**20),
    )(blocks, ids)
    slots = blocks.shape[0]
    return pl.pallas_call(
        local_kernel,
        out_shape=jax.ShapeDtypeStruct(blocks.shape, F32),
        in_specs=[
            pl.BlockSpec(memory_space=pltpu.SMEM), pl.BlockSpec(memory_space=pltpu.SMEM), anywhere, anywhere, anywhere,
        ],
        out_specs=anywhere,
        scratch_shapes=[
            vmem((slots, W, W), F32), vmem((2, 3 * PR, W, W), F32), vmem((6, W, W), F32),
            vmem((3 * PR, W, 4 * W), jnp.bfloat16), vmem((W, 9 * W), jnp.bfloat16), vmem((2, W, W), F32),
            pltpu.SMEM((slots,), jnp.int32), pltpu.SMEM((2 * PR * PR,), jnp.int32),
            dma((slots,)), dma, dma((2, 3)), dma,
        ],
        compiler_params=pltpu.CompilerParams(vmem_limit_bytes=60 * 2**20),
    )(ids, idb, blocks, buf, ch)


def solution(mesh):
    return jax.shard_map(
        on_device,
        mesh=mesh,
        in_specs=(P(("wide", "narrow"), None, None), P(("wide", "narrow"), None)),
        out_specs=P(("wide", "narrow"), None, None),
        check_vma=False,
    )
```
